256 devices in a mesh: dp: 16 (over z, core), cent: 16 (over x, y).
Axes of the slice: x: 4, y: 4, z: 8, core: 2. Of those that a mesh axis runs over, the one named last changes fastest.
Arguments:
- embeds: bfloat16 [24576, 1024], P('dp'), as said below
- centroids: bfloat16 [16384, 1024], P('cent'), as said below
Outputs:
- new_centroids: bfloat16 [16384, 1024], P('cent')
- row_lse: float32 [24576], P('dp')
Inputs may be any that keep to these rules, and one draw needn't show every extreme that they name: `centroids`: centroids lie within -0.6 to 0.6. `embeds`: embeddings lie within -6 to 6.
All inputs are finite; a program needn't handle non-finite values.
Results may differ from the reference program's by a relative error of at most 0.012.
The reference program's roundings to bfloat16 on the way (of `current` and `weights`) count: a program that leaves them out, or rounds other values in their place, can miss the bound.
Values may be sent and summed in bfloat16 or wider, within the bound.
A program may use at most 64 MiB of HBM per device.

```python
import jax
import jax.numpy as jnp
from jax import lax

D = 1024
ROWS_DEV = 1536
ITERS = 2
ROWS = 24576
CENTS = 16384


def sign_table(key):
    return jnp.where(jax.random.normal(jax.random.fold_in(key, 17), (CENTS, D), jnp.float32) > 0.0, 1.0, -1.0)


def centroid_table(key):
    values = jnp.clip(0.1 * jax.random.normal(jax.random.fold_in(key, 11), (CENTS, D), jnp.float32), -0.6, 0.6)
    signs = sign_table(key)
    rows = jnp.arange(CENTS, dtype=jnp.int32)[:, None]
    feats = jnp.arange(D, dtype=jnp.int32)[None, :]
    planted = (rows % 32 < 2) & (feats < 64)
    leader = rows - rows % 2
    lead_signs = jnp.take(signs, leader[:, 0], axis=0)
    magnitude = jnp.where((rows % 2 == 1) & (feats == 0), 0.3, 0.5)
    return jnp.where(planted, magnitude * lead_signs, values)


def draw_centroids(key, part):
    return centroid_table(key).astype(jnp.bfloat16)


def draw_embeds(key, part):
    base = jnp.clip(jax.random.normal(jax.random.fold_in(key, 23), (ROWS, D), jnp.float32), -6.0, 6.0)
    signs = sign_table(key)
    index = jnp.arange(ROWS, dtype=jnp.int32)
    picked = index % 61 == 0
    which = index // 61 * 32 % CENTS
    factor = (4 + index // 61 % 3).astype(jnp.float32)
    feats = jnp.arange(D, dtype=jnp.int32)[None, :]
    aligned = jnp.where(feats < 64, factor[:, None] * jnp.take(signs, which, axis=0), 0.0)
    return jnp.where(picked[:, None], aligned, base).astype(jnp.bfloat16)


def setup_inputs(seed: int = 0) -> dict:
    seeds = jax.random.split(jax.random.key(seed), 3)
    return {
        "embeds": draw_embeds(jax.random.fold_in(seeds[2], 71), 0),
        "centroids": draw_centroids(jax.random.fold_in(seeds[2], 71), 0),
    }


inverse_temp = 2.5


def reference(embeds, centroids):
    current = centroids
    blocks = ROWS // ROWS_DEV
    pieces = embeds.reshape(blocks, ROWS_DEV, D)
    last_lse = jnp.zeros((ROWS,), jnp.float32)
    for turn in range(ITERS):
        norms = jnp.sum(jnp.square(current.astype(jnp.float32)), axis=1)

        def one_block(carry, piece):
            sums, mass = carry
            scores = inverse_temp * (jnp.dot(piece, current.T, preferred_element_type=jnp.float32) - 0.5 * norms[None, :])
            top = jnp.max(scores, axis=1)
            lse = top + jnp.log(jnp.sum(jnp.exp(scores - top[:, None]), axis=1))
            weights = jnp.exp(scores - lse[:, None]).astype(jnp.bfloat16)
            sums = sums + lax.dot_general(weights, piece, (((0,), (0,)), ((), ())), preferred_element_type=jnp.float32)
            mass = mass + jnp.sum(weights.astype(jnp.float32), axis=0)
            return (sums, mass), lse

        start = (jnp.zeros((CENTS, D), jnp.float32), jnp.zeros((CENTS,), jnp.float32))
        (sums, mass), lses = lax.scan(one_block, start, pieces)
        last_lse = lses.reshape(ROWS)
        current = ((sums + current.astype(jnp.float32)) / (mass[:, None] + 1.0)).astype(jnp.bfloat16)
    return current, last_lse
```

```python
import functools
import math

import jax
import jax.numpy as jnp
from jax import lax
from jax.experimental import pallas as pl
from jax.experimental.pallas import tpu as pltpu
from jax.sharding import PartitionSpec as P

ITERS = 2
TEMP = 2.5
D = 1024
ROWS = 1536
CENTS = 1024
NZ = 8
NC = 16
OWN = CENTS // 2
CHUNK = OWN // NZ
HALF = CHUNK // 2
GROUP = OWN // 2
RB = 512
KEXP = TEMP * math.log2(math.e)
LN2 = math.log(2.0)

OFF = (4, 3, 5, 2, 6, 1, 7, 0)
SLOT = {o: j for j, o in enumerate(OFF)}
CHAINS = ((1, 0, 4), (-1, 1, 4), (1, 1, 3), (-1, 0, 3))
MSG = {}
for _c, (_d, _h, _l) in enumerate(CHAINS):
    for _k in range(_l):
        MSG[(_c, _k)] = len(MSG)
NMSG = len(MSG)
MESH = pl.DeviceIdType.MESH
F32 = jnp.float32
BF16 = jnp.bfloat16


def nt_dot(a, b):
    return lax.dot_general(a, b, (((1,), (1,)), ((), ())), preferred_element_type=F32)


def lse2(parts):
    top = functools.reduce(jnp.maximum, parts)
    return top + jnp.log2(sum(jnp.exp2(p - top) for p in parts))


def kernel(
    emb, cen, out, row_lse,
    E, CUR, CO, PB, W, SUMS, MG, LOC, XS, XR, SS, SR, MACC, MS, MR, RSB, RRB,
    ld_e, ld_c, es_s, es_r, x_s, x_r, s_s, s_r, m_s, m_r, rs_s, rs_r, ag_s, ag_r, o_l, o_s, o_r,
):
    dp = lax.axis_index("dp")
    cent = lax.axis_index("cent")
    z = dp // 2
    core = dp % 2
    sib = (z * 2 + (1 - core), cent)

    def zdev(h):
        return (((z + h + NZ) % NZ) * 2 + core, cent)

    def cdev(k):
        return (dp, (cent + k) % NC)

    def remote(src, dst, s, r, dev):
        return pltpu.make_async_remote_copy(
            src_ref=src, dst_ref=dst, send_sem=s, recv_sem=r, device_id=dev, device_id_type=MESH
        )

    def chunk_row(j):
        return pl.multiple_of(core * OWN + ((z + OFF[j]) % NZ) * CHUNK, CHUNK)

    barrier = pltpu.get_barrier_semaphore()
    pl.semaphore_signal(barrier, inc=1, device_id=sib, device_id_type=MESH)
    for k in range(1, NC):
        pl.semaphore_signal(barrier, inc=1, device_id=cdev(k), device_id_type=MESH)
    for h in range(1, NZ):
        pl.semaphore_signal(barrier, inc=1, device_id=zdev(h), device_id_type=MESH)

    load_c = [
        pltpu.make_async_copy(cen.at[pl.ds(chunk_row(j), CHUNK)], CUR.at[0, pl.ds(j * CHUNK, CHUNK)], ld_c.at[j])
        for j in range(NZ)
    ]
    load_c.append(
        pltpu.make_async_copy(cen.at[pl.ds(pl.multiple_of((1 - core) * OWN, OWN), OWN)], CO, ld_c.at[NZ])
    )
    nb = ROWS // RB
    load_e = [
        pltpu.make_async_copy(emb.at[pl.ds(b * RB, RB)], E.at[pl.ds(b * RB, RB)], ld_e.at[b]) for b in range(nb)
    ]
    for c in load_c[:NZ]:
        c.start()
    load_e[0].start()
    load_c[NZ].start()
    for c in load_e[1:]:
        c.start()

    pl.semaphore_wait(barrier, NC - 1 + NZ - 1 + 1)
    send_e = [
        remote(emb.at[pl.ds(b * RB, RB)], E.at[pl.ds(ROWS + b * RB, RB)], es_s.at[b], es_r.at[b], sib)
        for b in range(nb)
    ]
    for c in send_e:
        c.start()
    for c in load_c:
        c.wait()
    for c in load_e:
        c.wait()

    def half_norm(c):
        return (0.5 * KEXP) * jnp.sum(jnp.square(c.astype(F32)), axis=1, keepdims=True)

    def block(c, n, r0):
        s = KEXP * nt_dot(c, E[pl.ds(r0, RB), :]) - n
        m = jnp.max(s, axis=0, keepdims=True)
        p = jnp.exp2(s - m)
        return p, m, m + jnp.log2(jnp.sum(p, axis=0, keepdims=True))

    def own_groups(turn, r0):
        lses = []
        for g in range(2):
            c = CUR[turn, pl.ds(g * GROUP, GROUP), :]
            p, m, l = block(c, half_norm(c), r0)
            PB[pl.ds(g * GROUP, GROUP), pl.ds(r0, RB)] = p
            MG[g, :, pl.ds(r0, RB)] = m
            lses.append(l)
        return lses

    for turn in range(ITERS):
        if turn == 0:

            @pl.loop(0, nb)
            def _(b):
                r0 = pl.multiple_of(b * RB, RB)
                lses = own_groups(0, r0)
                for g in range(2):
                    c = CO[pl.ds(g * GROUP, GROUP), :]
                    lses.append(block(c, half_norm(c), r0)[2])
                XS[turn, :, pl.ds(r0, RB)] = lse2(lses)

        else:

            @pl.loop(nb, 2 * nb)
            def _(b):
                r0 = pl.multiple_of(b * RB, RB)
                LOC[:, pl.ds(r0, RB)] = lse2(own_groups(turn, r0))

            part = remote(LOC.at[:, pl.ds(ROWS, ROWS)], SR.at[0], s_s.at[0], s_r.at[0], sib)
            part.start()

            @pl.loop(0, nb)
            def _(b):
                r0 = pl.multiple_of(b * RB, RB)
                LOC[:, pl.ds(r0, RB)] = lse2(own_groups(turn, r0))

            part.wait()
            XS[turn] = lse2([LOC[:, pl.ds(0, ROWS)], SR[0]])

        sends = [
            remote(XS.at[turn], XR.at[turn, k - 1], x_s.at[turn, k - 1], x_r.at[turn, k - 1], cdev(k))
            for k in range(1, NC)
        ]
        for c in sends:
            c.start()
        if turn == 0:
            for c in send_e:
                c.wait()

            @pl.loop(nb, 2 * nb)
            def _(b):
                own_groups(0, pl.multiple_of(b * RB, RB))

        for c in sends:
            c.wait()
        total = lse2([XS[turn]] + [XR[turn, k] for k in range(NC - 1)])
        SS[turn] = total
        LOC[:, pl.ds(0, ROWS)] = total
        back = remote(SS.at[turn], SR.at[1 + turn], s_s.at[1 + turn], s_r.at[1 + turn], sib)
        back.start()
        if turn == ITERS - 1:
            row_lse[...] = total * LN2

        MACC[...] = jnp.zeros_like(MACC)

        def weights(b):
            r0 = pl.multiple_of(b * RB, RB)
            lse = LOC[:, pl.ds(r0, RB)]
            for g in range(2):
                rows = pl.ds(g * GROUP, GROUP)
                w = (PB[rows, pl.ds(r0, RB)] * jnp.exp2(MG[g, :, pl.ds(r0, RB)] - lse)).astype(BF16)
                W[rows, pl.ds(r0, RB)] = w
                wf = w.astype(F32)
                MACC[rows, :] += sum(wf[:, i * 128 : (i + 1) * 128] for i in range(RB // 128))

        pl.loop(0, nb)(weights)
        back.wait()
        LOC[:, pl.ds(ROWS, ROWS)] = SR[1 + turn]
        pl.loop(nb, 2 * nb)(weights)
        MS[turn] = jnp.sum(MACC[...].T, axis=0, keepdims=True)
        masses = [
            remote(MS.at[turn], MR.at[turn, h - 1], m_s.at[turn, h - 1], m_r.at[turn, h - 1], zdev(h))
            for h in range(1, NZ)
        ]
        for c in masses:
            c.start()

        for g in range(2):

            @pl.loop(0, D // 256)
            def _(n):
                cols = pl.ds(pl.multiple_of(n * 256, 256), 256)
                SUMS[pl.ds(g * GROUP, GROUP), cols] = jnp.dot(
                    W[pl.ds(g * GROUP, GROUP), :], E[:, cols], preferred_element_type=F32
                )

        ring = {
            (c, k): remote(
                RSB.at[turn, MSG[c, k]], RRB.at[turn, MSG[c, k]],
                rs_s.at[turn, MSG[c, k]], rs_r.at[turn, MSG[c, k]], zdev(CHAINS[c][0]),
            )
            for c, k in MSG
        }
        for k in range(4):
            for c, (d, h, hops) in enumerate(CHAINS):
                if k < hops:
                    o = (d * (hops - k)) % NZ
                    v = SUMS[pl.ds(SLOT[o] * CHUNK + h * HALF, HALF), :]
                    if k:
                        ring[c, k - 1].wait_recv()
                        v = v + RRB[turn, MSG[c, k - 1]].astype(F32)
                    RSB[turn, MSG[c, k]] = v.astype(BF16)
                    ring[c, k].start()
        for c in masses:
            c.wait()
        lane = lax.broadcasted_iota(jnp.int32, (CHUNK, 128), 1)
        row = lax.broadcasted_iota(jnp.int32, (CHUNK, 128), 0)
        acc = jnp.zeros((CHUNK, 128), F32)
        for h in range(NZ):
            j = SLOT[h]
            vec = MS[turn] if h == 0 else MR[turn, h - 1]
            vec = vec[:, (j // 2) * 128 : (j // 2 + 1) * 128]
            acc = acc + jnp.where(lane == row + CHUNK * (j % 2), jnp.broadcast_to(vec, (CHUNK, 128)), 0.0)
        inv = 1.0 / (jnp.sum(acc, axis=1, keepdims=True) + 1.0)

        gather = {}
        for c, (d, h, hops) in enumerate(CHAINS):
            for k in range(hops):
                src = CUR.at[turn + 1, pl.ds(SLOT[(-d * k) % NZ] * CHUNK + h * HALF, HALF)]
                dst = CUR.at[turn + 1, pl.ds(SLOT[(-d * (k + 1)) % NZ] * CHUNK + h * HALF, HALF)]
                i = MSG[c, k]
                gather[c, k] = remote(src, dst, ag_s.at[turn, i], ag_r.at[turn, i], zdev(d))
        last_hop = {0: ((0, 3), (3, 2)), 1: ((1, 3), (2, 2))}
        for h in range(2):
            rows = pl.ds(SLOT[0] * CHUNK + h * HALF, HALF)
            v = SUMS[rows, :] + CUR[turn, rows, :].astype(F32)
            for c, k in last_hop[h]:
                ring[c, k].wait_recv()
                v = v + RRB[turn, MSG[c, k]].astype(F32)
            CUR[turn + 1, rows, :] = (v * inv[h * HALF : (h + 1) * HALF]).astype(BF16)
            for c in range(4):
                if CHAINS[c][1] == h:
                    gather[c, 0].start()
        for k in range(1, 4):
            for c, (d, h, hops) in enumerate(CHAINS):
                if k < hops:
                    gather[c, k - 1].wait_recv()
                    gather[c, k].start()
        for c, (d, h, hops) in enumerate(CHAINS):
            gather[c, hops - 1].wait_recv()
        for c, k in MSG:
            ring[c, k].wait_send()
            gather[c, k].wait_send()

    stores = []
    for j in range(NZ):
        src = CUR.at[ITERS, pl.ds(j * CHUNK, CHUNK)]
        dst = out.at[pl.ds(chunk_row(j), CHUNK)]
        stores.append(pltpu.make_async_copy(src, dst, o_l.at[j]))
        stores.append(remote(src, dst, o_s.at[j], o_r.at[j], sib))
    for c in stores:
        c.start()
    for c in stores:
        c.wait()


def per_device(embeds, centroids):
    dma = pltpu.SemaphoreType.DMA
    new, lse = pl.pallas_call(
        kernel,
        out_shape=(
            jax.ShapeDtypeStruct((CENTS, D), BF16),
            jax.ShapeDtypeStruct((1, ROWS), F32),
        ),
        in_specs=[pl.BlockSpec(memory_space=pl.ANY)] * 2,
        out_specs=(pl.BlockSpec(memory_space=pl.ANY), pl.BlockSpec(memory_space=pltpu.VMEM)),
        scratch_shapes=[
            pltpu.VMEM((2 * ROWS, D), BF16),
            pltpu.VMEM((ITERS + 1, OWN, D), BF16),
            pltpu.VMEM((OWN, D), BF16),
            pltpu.VMEM((OWN, 2 * ROWS), F32),
            pltpu.VMEM((OWN, 2 * ROWS), BF16),
            pltpu.VMEM((OWN, D), F32),
            pltpu.VMEM((2, 1, 2 * ROWS), F32),
            pltpu.VMEM((1, 2 * ROWS), F32),
            pltpu.VMEM((ITERS, 1, ROWS), F32),
            pltpu.VMEM((ITERS, NC - 1, 1, ROWS), F32),
            pltpu.VMEM((ITERS, 1, ROWS), F32),
            pltpu.VMEM((ITERS + 1, 1, ROWS), F32),
            pltpu.VMEM((OWN, 128), F32),
            pltpu.VMEM((ITERS, 1, OWN), F32),
            pltpu.VMEM((ITERS, NZ - 1, 1, OWN), F32),
            pltpu.VMEM((ITERS, NMSG, HALF, D), BF16),
            pltpu.VMEM((ITERS, NMSG, HALF, D), BF16),
            dma((ROWS // RB,)),
            dma((NZ + 1,)),
            dma((ROWS // RB,)),
            dma((ROWS // RB,)),
            dma((ITERS, NC - 1)),
            dma((ITERS, NC - 1)),
            dma((ITERS + 1,)),
            dma((ITERS + 1,)),
            dma((ITERS, NZ - 1)),
            dma((ITERS, NZ - 1)),
            dma((ITERS, NMSG)),
            dma((ITERS, NMSG)),
            dma((ITERS, NMSG)),
            dma((ITERS, NMSG)),
            dma((NZ,)),
            dma((NZ,)),
            dma((NZ,)),
        ],
        compiler_params=pltpu.CompilerParams(
            collective_id=0, has_side_effects=True, vmem_limit_bytes=56 * 1024 * 1024
        ),
    )(embeds, centroids)
    return new, lse.reshape(ROWS)


def solution(mesh):
    return jax.shard_map(
        per_device,
        mesh=mesh,
        in_specs=(P("dp", None), P("cent", None)),
        out_specs=(P("cent", None), P("dp")),
        check_vma=False,
    )
```

```python
import functools
import math

import jax
import jax.numpy as jnp
from jax import lax
from jax.experimental import pallas as pl
from jax.experimental.pallas import tpu as pltpu
from jax.sharding import PartitionSpec as P

ITERS = 2
TEMP = 2.5
D = 1024
ROWS = 1536
CENTS = 1024
NZ = 8
NC = 16
OWN = CENTS // 2
CHUNK = OWN // NZ
WAVES = 2
PIECE = CHUNK // WAVES // 2
GROUP = OWN // 2
RB = 512
NB = ROWS // RB
KEXP = TEMP * math.log2(math.e)
LN2 = math.log(2.0)

OFF = (4, 3, 5, 2, 6, 1, 7, 0)
SLOT = {o: j for j, o in enumerate(OFF)}
CHAINS = ((1, 0, 4), (-1, 1, 4), (1, 1, 3), (-1, 0, 3))
MSG = {}
for _w in range(WAVES):
    for _c, (_d, _h, _l) in enumerate(CHAINS):
        for _k in range(_l):
            MSG[(_w, _c, _k)] = len(MSG)
NMSG = len(MSG)
MESH = pl.DeviceIdType.MESH
F32 = jnp.float32
BF16 = jnp.bfloat16


def nt_dot(a, b):
    return lax.dot_general(a, b, (((1,), (1,)), ((), ())), preferred_element_type=F32)


def lse2(parts):
    top = functools.reduce(jnp.maximum, parts)
    return top + jnp.log2(sum(jnp.exp2(p - top) for p in parts))


def kernel(
    emb, cen, out, row_lse,
    E, CUR, CO, NRM, NRO, PB, W, SUMS, MG, LG, LOC, XS, XR, SS, SR, MACC, MS, MR, RSB, RRB,
    ld_e, ld_c, es_s, es_r, x_s, x_r, s_s, s_r, m_s, m_r, rs_s, rs_r, ag_s, ag_r, o_l, o_s, o_r,
):
    dp = lax.axis_index("dp")
    cent = lax.axis_index("cent")
    z = dp // 2
    core = dp % 2
    sib = (z * 2 + (1 - core), cent)

    def zdev(h):
        return (((z + h + NZ) % NZ) * 2 + core, cent)

    def cdev(k):
        return (dp, (cent + k) % NC)

    def remote(src, dst, s, r, dev):
        return pltpu.make_async_remote_copy(
            src_ref=src, dst_ref=dst, send_sem=s, recv_sem=r, device_id=dev, device_id_type=MESH
        )

    def chunk_row(j):
        return pl.multiple_of(core * OWN + ((z + OFF[j]) % NZ) * CHUNK, CHUNK)

    barrier = pltpu.get_barrier_semaphore()
    pl.semaphore_signal(barrier, inc=1, device_id=sib, device_id_type=MESH)
    for k in range(1, NC):
        pl.semaphore_signal(barrier, inc=1, device_id=cdev(k), device_id_type=MESH)
    for h in range(1, NZ):
        pl.semaphore_signal(barrier, inc=1, device_id=zdev(h), device_id_type=MESH)

    load_c = [
        pltpu.make_async_copy(cen.at[pl.ds(chunk_row(j), CHUNK)], CUR.at[0, pl.ds(j * CHUNK, CHUNK)], ld_c.at[j])
        for j in range(NZ)
    ]
    load_c.append(
        pltpu.make_async_copy(cen.at[pl.ds(pl.multiple_of((1 - core) * OWN, OWN), OWN)], CO, ld_c.at[NZ])
    )
    load_e = [
        pltpu.make_async_copy(emb.at[pl.ds(b * RB, RB)], E.at[pl.ds(b * RB, RB)], ld_e.at[b]) for b in range(NB)
    ]
    for c in load_c[:NZ]:
        c.start()
    load_e[0].start()
    load_c[NZ].start()
    for c in load_e[1:]:
        c.start()

    pl.semaphore_wait(barrier, NC - 1 + NZ - 1 + 1)
    send_e = [
        remote(emb.at[pl.ds(b * RB, RB)], E.at[pl.ds(ROWS + b * RB, RB)], es_s.at[b], es_r.at[b], sib)
        for b in range(NB)
    ]
    for c in send_e:
        c.start()
    for c in load_c:
        c.wait()
    for c in load_e:
        c.wait()

    def store_norms(turn, g):
        c = CUR[turn, pl.ds(g * GROUP, GROUP), :]
        n = (0.5 * KEXP) * jnp.sum(jnp.square(c.astype(F32)), axis=1, keepdims=True)
        NRM[pl.ds(g * GROUP, GROUP), :] = jnp.broadcast_to(n, (GROUP, 128))

    def block(c, n, r0):
        s = KEXP * nt_dot(c, E[pl.ds(r0, RB), :]) - n
        m = jnp.max(s, axis=0, keepdims=True)
        p = jnp.exp2(s - m)
        return p, m, m + jnp.log2(jnp.sum(p, axis=0, keepdims=True))

    def wide(n):
        return jnp.concatenate([n] * (RB // 128), axis=1)

    def own_block(turn, g, b):
        r0 = pl.multiple_of(b * RB, RB)
        rows, cols = pl.ds(g * GROUP, GROUP), pl.ds(r0, RB)
        n = wide(NRM[rows, :])
        p, m, l = block(CUR[turn, rows, :], n, r0)
        PB[rows, cols] = p
        MG[g, :, cols] = m
        LG[g, :, cols] = l

    for g in range(2):
        store_norms(0, g)
        c = CO[pl.ds(g * GROUP, GROUP), :]
        n = (0.5 * KEXP) * jnp.sum(jnp.square(c.astype(F32)), axis=1, keepdims=True)
        NRO[pl.ds(g * GROUP, GROUP), :] = jnp.broadcast_to(n, (GROUP, 128))
    mine, theirs = pl.ds(0, ROWS), pl.ds(ROWS, ROWS)

    for turn in range(ITERS):
        last = turn == ITERS - 1
        if turn == 0:

            @pl.loop(0, NB)
            def _(b):
                r0 = pl.multiple_of(b * RB, RB)
                for g in range(2):
                    own_block(0, g, b)
                lses = [LG[g, :, pl.ds(r0, RB)] for g in range(2)]
                for g in range(2):
                    rows = pl.ds(g * GROUP, GROUP)
                    lses.append(block(CO[rows, :], wide(NRO[rows, :]), r0)[2])
                XS[turn, :, pl.ds(r0, RB)] = lse2(lses)

        else:
            pl.loop(NB, 2 * NB)(functools.partial(own_block, turn, 0))
            LOC[:, theirs] = lse2([LG[0, :, theirs], LG[1, :, theirs]])
            part = remote(LOC.at[:, theirs], SR.at[0], s_s.at[0], s_r.at[0], sib)
            part.start()
            pl.loop(0, NB)(functools.partial(own_block, turn, 0))
            both = lse2([LG[0, :, mine], LG[1, :, mine]])
            part.wait()
            XS[turn] = lse2([both, SR[0]])

        sends = [
            remote(XS.at[turn], XR.at[turn, k - 1], x_s.at[turn, k - 1], x_r.at[turn, k - 1], cdev(k))
            for k in range(1, NC)
        ]
        for c in sends:
            c.start()
        if turn == 0:
            for c in send_e:
                c.wait()

            @pl.loop(NB, 2 * NB)
            def _(b):
                for g in range(2):
                    own_block(0, g, b)

        for c in sends:
            c.wait()
        total = lse2([XS[turn]] + [XR[turn, k] for k in range(NC - 1)])
        SS[turn] = total
        LOC[:, mine] = total
        back = remote(SS.at[turn], SR.at[1 + turn], s_s.at[1 + turn], s_r.at[1 + turn], sib)
        back.start()
        MACC[...] = jnp.zeros_like(MACC)

        def weights(b):
            r0 = pl.multiple_of(b * RB, RB)
            lse = LOC[:, pl.ds(r0, RB)]
            for g in range(2):
                rows = pl.ds(g * GROUP, GROUP)
                w = (PB[rows, pl.ds(r0, RB)] * jnp.exp2(MG[g, :, pl.ds(r0, RB)] - lse)).astype(BF16)
                W[rows, pl.ds(r0, RB)] = w
                wf = w.astype(F32)
                MACC[rows, :] += sum(wf[:, i * 128 : (i + 1) * 128] for i in range(RB // 128))

        pl.loop(0, NB)(weights)
        back.wait()
        LOC[:, theirs] = SR[1 + turn]
        pl.loop(NB, 2 * NB)(weights)

        def sums(g):
            @pl.loop(0, D // 256)
            def _(n):
                cols = pl.ds(pl.multiple_of(n * 256, 256), 256)
                SUMS[pl.ds(g * GROUP, GROUP), cols] = jnp.dot(
                    W[pl.ds(g * GROUP, GROUP), :], E[:, cols], preferred_element_type=F32
                )

        ring = {
            (w, c, k): remote(
                RSB.at[turn, i], RRB.at[turn, i], rs_s.at[turn, i], rs_r.at[turn, i], zdev(CHAINS[c][0])
            )
            for (w, c, k), i in MSG.items()
        }

        def ring_hop(w, k):
            for c, (d, h, hops) in enumerate(CHAINS):
                if k < hops:
                    o = (d * (hops - k)) % NZ
                    v = SUMS[pl.ds(SLOT[o] * CHUNK + (2 * w + h) * PIECE, PIECE), :]
                    if k:
                        ring[w, c, k - 1].wait_recv()
                        v = v + RRB[turn, MSG[w, c, k - 1]].astype(F32)
                    RSB[turn, MSG[w, c, k]] = v.astype(BF16)
                    ring[w, c, k].start()

        sums(0)
        for w in range(WAVES):
            ring_hop(w, 0)
        sums(1)
        MS[turn] = jnp.sum(MACC[...].T, axis=0, keepdims=True)
        masses = [
            remote(MS.at[turn], MR.at[turn, h - 1], m_s.at[turn, h - 1], m_r.at[turn, h - 1], zdev(h))
            for h in range(1, NZ)
        ]
        for c in masses:
            c.start()
        for k in range(1, 4):
            for w in range(WAVES):
                ring_hop(w, k)
        for c in masses:
            c.wait()
        lane = lax.broadcasted_iota(jnp.int32, (CHUNK, 128), 1)
        row = lax.broadcasted_iota(jnp.int32, (CHUNK, 128), 0)
        acc = jnp.zeros((CHUNK, 128), F32)
        for h in range(NZ):
            j = SLOT[h]
            vec = MS[turn] if h == 0 else MR[turn, h - 1]
            vec = vec[:, (j // 2) * 128 : (j // 2 + 1) * 128]
            acc = acc + jnp.where(lane == row + CHUNK * (j % 2), jnp.broadcast_to(vec, (CHUNK, 128)), 0.0)
        inv = 1.0 / (jnp.sum(acc, axis=1, keepdims=True) + 1.0)

        def place(o, piece):
            start = piece * PIECE
            if last:
                return out.at[pl.ds(pl.multiple_of(chunk_row(SLOT[o % NZ]) + start, PIECE), PIECE)]
            return CUR.at[turn + 1, pl.ds(SLOT[o % NZ] * CHUNK + start, PIECE)]

        gather, pairs, keeps = {}, {}, []
        for (w, c, k), i in MSG.items():
            d, h, hops = CHAINS[c]
            piece = 2 * w + h
            src = place(-d * k, piece)
            dst = src if last else place(-d * (k + 1), piece)
            if last and k == 0:
                src = CUR.at[0, pl.ds(piece * PIECE, PIECE)]
            gather[w, c, k] = remote(src, dst, ag_s.at[turn, i], ag_r.at[turn, i], zdev(d))
            if last:
                got = place(-d * (k + 1), 2 * w + h)
                pairs[w, c, k] = remote(got, got, o_s.at[i], o_r.at[i], sib)
        if last:
            for w in range(WAVES):
                start = 2 * w * PIECE
                fresh = CUR.at[0, pl.ds(start, 2 * PIECE)]
                rows = out.at[pl.ds(pl.multiple_of(chunk_row(SLOT[0]) + start, 2 * PIECE), 2 * PIECE)]
                pairs[w] = remote(fresh, rows, o_s.at[NMSG + w], o_r.at[NMSG + w], sib)
                keeps.append(pltpu.make_async_copy(fresh, rows, o_l.at[w]))

        def finish(w):
            for h in range(2):
                piece = 2 * w + h
                rows = pl.ds(SLOT[0] * CHUNK + piece * PIECE, PIECE)
                v = SUMS[rows, :] + CUR[turn, rows, :].astype(F32)
                for c in range(4):
                    if CHAINS[c][1] == h:
                        k = CHAINS[c][2] - 1
                        ring[w, c, k].wait_recv()
                        v = v + RRB[turn, MSG[w, c, k]].astype(F32)
                fresh = (v * inv[piece * PIECE : (piece + 1) * PIECE]).astype(BF16)
                if last:
                    CUR[0, pl.ds(piece * PIECE, PIECE), :] = fresh
                else:
                    CUR[turn + 1, rows, :] = fresh
                for c in range(4):
                    if CHAINS[c][1] == h:
                        gather[w, c, 0].start()
            if last:
                pairs[w].start()
                keeps[w].start()

        def gather_hop(w, k):
            for c, (d, h, hops) in enumerate(CHAINS):
                if k <= hops:
                    gather[w, c, k - 1].wait_recv()
                    if k < hops:
                        gather[w, c, k].start()
                    if last:
                        pairs[w, c, k - 1].start()

        for w in range(WAVES):
            finish(w)
        for k in (1, 2):
            for w in range(WAVES):
                gather_hop(w, k)
        if last:
            for k in (3, 4):
                for w in range(WAVES):
                    gather_hop(w, k)
            row_lse[...] = (SS[turn] * LN2).reshape(ROWS)
        else:
            store_norms(turn + 1, 1)
            near = functools.partial(own_block, turn + 1, 1)
            pl.loop(0, 2)(near)
            gather_hop(0, 3)
            gather_hop(1, 3)
            pl.loop(2, 4)(near)
            gather_hop(0, 4)
            gather_hop(1, 4)
            pl.loop(4, 6)(near)
            store_norms(turn + 1, 0)
        for key in MSG:
            ring[key].wait_send()
            gather[key].wait_send()

    for c in list(pairs.values()) + keeps:
        c.wait()


def per_device(embeds, centroids):
    dma = pltpu.SemaphoreType.DMA
    new, lse = pl.pallas_call(
        kernel,
        out_shape=(
            jax.ShapeDtypeStruct((CENTS, D), BF16),
            jax.ShapeDtypeStruct((ROWS,), F32),
        ),
        in_specs=[pl.BlockSpec(memory_space=pltpu.HBM)] * 2,
        out_specs=(pl.BlockSpec(memory_space=pl.ANY), pl.BlockSpec(memory_space=pltpu.VMEM)),
        scratch_shapes=[
            pltpu.VMEM((2 * ROWS, D), BF16),
            pltpu.VMEM((ITERS, OWN, D), BF16),
            pltpu.VMEM((OWN, D), BF16),
            pltpu.VMEM((OWN, 128), F32),
            pltpu.VMEM((OWN, 128), F32),
            pltpu.VMEM((OWN, 2 * ROWS), F32),
            pltpu.VMEM((OWN, 2 * ROWS), BF16),
            pltpu.VMEM((OWN, D), F32),
            pltpu.VMEM((2, 1, 2 * ROWS), F32),
            pltpu.VMEM((2, 1, 2 * ROWS), F32),
            pltpu.VMEM((1, 2 * ROWS), F32),
            pltpu.VMEM((ITERS, 1, ROWS), F32),
            pltpu.VMEM((ITERS, NC - 1, 1, ROWS), F32),
            pltpu.VMEM((ITERS, 1, ROWS), F32),
            pltpu.VMEM((ITERS + 1, 1, ROWS), F32),
            pltpu.VMEM((OWN, 128), F32),
            pltpu.VMEM((ITERS, 1, OWN), F32),
            pltpu.VMEM((ITERS, NZ - 1, 1, OWN), F32),
            pltpu.VMEM((ITERS, NMSG, PIECE, D), BF16),
            pltpu.VMEM((ITERS, NMSG, PIECE, D), BF16),
            dma((ROWS // RB,)),
            dma((NZ + 1,)),
            dma((ROWS // RB,)),
            dma((ROWS // RB,)),
            dma((ITERS, NC - 1)),
            dma((ITERS, NC - 1)),
            dma((ITERS + 1,)),
            dma((ITERS + 1,)),
            dma((ITERS, NZ - 1)),
            dma((ITERS, NZ - 1)),
            dma((ITERS, NMSG)),
            dma((ITERS, NMSG)),
            dma((ITERS, NMSG)),
            dma((ITERS, NMSG)),
            dma((WAVES,)),
            dma((NMSG + WAVES,)),
            dma((NMSG + WAVES,)),
        ],
        compiler_params=pltpu.CompilerParams(
            collective_id=0, has_side_effects=True, vmem_limit_bytes=50 * 1024 * 1024
        ),
    )(embeds, centroids)
    return new, lse


def solution(mesh):
    return jax.shard_map(
        per_device,
        mesh=mesh,
        in_specs=(P("dp", None), P("cent", None)),
        out_specs=(P("cent", None), P("dp")),
        check_vma=False,
    )
```

```python
import functools
import math

import jax
import jax.numpy as jnp
from jax import lax
from jax.experimental import pallas as pl
from jax.experimental.pallas import tpu as pltpu
from jax.sharding import PartitionSpec as P

ITERS = 2
TEMP = 2.5
D = 1024
ROWS = 1536
CENTS = 1024
NZ = 8
NC = 16
OWN = CENTS // 2
CHUNK = OWN // NZ
WAVES = 2
PIECE = CHUNK // WAVES // 2
GROUP = OWN // 2
RB = 768
NB = ROWS // RB
KEXP = TEMP * math.log2(math.e)
LN2 = math.log(2.0)

OFF = (4, 3, 5, 2, 6, 1, 7, 0)
SLOT = {o: j for j, o in enumerate(OFF)}
CHAINS = ((1, 0, 4), (-1, 1, 4), (1, 1, 3), (-1, 0, 3))
MSG = {}
for _w in range(WAVES):
    for _c, (_d, _h, _l) in enumerate(CHAINS):
        for _k in range(_l):
            MSG[(_w, _c, _k)] = len(MSG)
NMSG = len(MSG)
MESH = pl.DeviceIdType.MESH
F32 = jnp.float32
BF16 = jnp.bfloat16


def nt_dot(a, b):
    return lax.dot_general(a, b, (((1,), (1,)), ((), ())), preferred_element_type=F32)


def lse2(parts):
    top = functools.reduce(jnp.maximum, parts)
    return top + jnp.log2(sum(jnp.exp2(p - top) for p in parts))


def kernel(
    emb, cen, out, row_lse,
    E, CUR, CO, NRM, NRO, PB, W, SUMS, SB, MG, LG, LOC, XS, XR, SS, SR, MACC, MS, MR, RSB, RRB,
    ld_e, ld_c, es_s, es_r, x_s, x_r, s_s, s_r, m_s, m_r, rs_s, rs_r, ag_s, ag_r, o_l, o_s, o_r,
):
    dp = lax.axis_index("dp")
    cent = lax.axis_index("cent")
    z = dp // 2
    core = dp % 2
    sib = (z * 2 + (1 - core), cent)

    def zdev(h):
        return (((z + h + NZ) % NZ) * 2 + core, cent)

    def cdev(k):
        return (dp, (cent + k) % NC)

    def remote(src, dst, s, r, dev):
        return pltpu.make_async_remote_copy(
            src_ref=src, dst_ref=dst, send_sem=s, recv_sem=r, device_id=dev, device_id_type=MESH
        )

    def chunk_row(j):
        return pl.multiple_of(core * OWN + ((z + OFF[j]) % NZ) * CHUNK, CHUNK)

    barrier = pltpu.get_barrier_semaphore()
    pl.semaphore_signal(barrier, inc=1, device_id=sib, device_id_type=MESH)
    for k in range(1, NC):
        pl.semaphore_signal(barrier, inc=1, device_id=cdev(k), device_id_type=MESH)
    for h in range(1, NZ):
        pl.semaphore_signal(barrier, inc=1, device_id=zdev(h), device_id_type=MESH)

    load_c = [
        pltpu.make_async_copy(cen.at[pl.ds(chunk_row(j), CHUNK)], CUR.at[0, pl.ds(j * CHUNK, CHUNK)], ld_c.at[j])
        for j in range(NZ)
    ]
    load_c.append(
        pltpu.make_async_copy(cen.at[pl.ds(pl.multiple_of((1 - core) * OWN, OWN), OWN)], CO, ld_c.at[NZ])
    )
    load_e = [
        pltpu.make_async_copy(emb.at[pl.ds(b * RB, RB)], E.at[pl.ds(b * RB, RB)], ld_e.at[b]) for b in range(NB)
    ]
    for c in load_c[:NZ]:
        c.start()
    load_e[0].start()
    load_c[NZ].start()
    for c in load_e[1:]:
        c.start()
    send_e = [
        remote(emb.at[pl.ds(b * RB, RB)], E.at[pl.ds(ROWS + b * RB, RB)], es_s.at[b], es_r.at[b], sib)
        for b in range(NB)
    ]

    def meet():
        pl.semaphore_wait(barrier, NC - 1 + NZ - 1 + 1)
        for c in send_e:
            c.start()

    def store_norms(dst, src, g):
        rows = pl.ds(g * GROUP, GROUP)
        n = (0.5 * KEXP) * jnp.sum(jnp.square(src[rows, :].astype(F32)), axis=1, keepdims=True)
        dst[rows, :] = jnp.broadcast_to(n, (GROUP, 128))

    def run_scores(items, hooks):
        def product(i):
            if i in hooks:
                hooks[i]()
            c, _, g, r0, _, _ = items[i]
            SB[i % 2] = nt_dot(c[pl.ds(g * GROUP, GROUP), :], E[pl.ds(r0, RB), :])

        product(0)
        for i, (_, norms, g, r0, slot, keep) in enumerate(items):
            if i + 1 < len(items):
                product(i + 1)
            rows, cols = pl.ds(g * GROUP, GROUP), pl.ds(r0, RB)
            s = KEXP * SB[i % 2] - jnp.concatenate([norms[rows, :]] * (RB // 128), axis=1)
            m = jnp.max(s, axis=0, keepdims=True)
            p = jnp.exp2(s - m)
            LG[slot, :, cols] = m + jnp.log2(jnp.sum(p, axis=0, keepdims=True))
            if keep:
                PB[rows, cols] = p
                MG[g, :, cols] = m

    def own_items(turn, groups, starts):
        return [(CUR.at[turn], NRM, g, r0, g, True) for r0 in starts for g in groups]

    mine_at, theirs_at = range(0, ROWS, RB), range(ROWS, 2 * ROWS, RB)
    for c in load_c:
        c.wait()
    for g in range(2):
        store_norms(NRM, CUR.at[0], g)
        store_norms(NRO, CO, g)
    load_e[0].wait()
    mine, theirs = pl.ds(0, ROWS), pl.ds(ROWS, ROWS)

    for turn in range(ITERS):
        last = turn == ITERS - 1
        if turn == 0:
            items = []
            for r0 in mine_at:
                items += own_items(0, range(2), [r0])
                items += [(CO, NRO, g, r0, 2 + g, False) for g in range(2)]
            run_scores(items, {2: meet, 4: load_e[1].wait})
            XS[turn] = lse2([LG[i, :, mine] for i in range(4)])
        else:
            run_scores(own_items(turn, [0], theirs_at), {})
            LOC[:, theirs] = lse2([LG[0, :, theirs], LG[1, :, theirs]])
            part = remote(LOC.at[:, theirs], SR.at[0], s_s.at[0], s_r.at[0], sib)
            part.start()
            run_scores(own_items(turn, [0], mine_at), {})
            both = lse2([LG[0, :, mine], LG[1, :, mine]])
            part.wait()
            XS[turn] = lse2([both, SR[0]])

        sends = [
            remote(XS.at[turn], XR.at[turn, k - 1], x_s.at[turn, k - 1], x_r.at[turn, k - 1], cdev(k))
            for k in range(1, NC)
        ]
        for c in sends:
            c.start()
        if turn == 0:
            send_e[0].wait()
            run_scores(own_items(0, range(2), theirs_at), {2: send_e[1].wait})

        for c in sends:
            c.wait()
        total = lse2([XS[turn]] + [XR[turn, k] for k in range(NC - 1)])
        SS[turn] = total
        LOC[:, mine] = total
        back = remote(SS.at[turn], SR.at[1 + turn], s_s.at[1 + turn], s_r.at[1 + turn], sib)
        back.start()
        MACC[...] = jnp.zeros_like(MACC)

        def weights(r0):
            lse = LOC[:, pl.ds(r0, RB)]
            for g in range(2):
                rows = pl.ds(g * GROUP, GROUP)
                w = (PB[rows, pl.ds(r0, RB)] * jnp.exp2(MG[g, :, pl.ds(r0, RB)] - lse)).astype(BF16)
                W[rows, pl.ds(r0, RB)] = w
                wf = w.astype(F32)
                MACC[rows, :] += sum(wf[:, i * 128 : (i + 1) * 128] for i in range(RB // 128))

        def sums(q, depth, add=False):
            rows = pl.ds(q * 2 * CHUNK, 2 * CHUNK)
            v = jnp.dot(W[rows, depth], E[depth, :], preferred_element_type=F32)
            SUMS[rows, :] = SUMS[rows, :] + v if add else v

        for r0 in mine_at:
            weights(r0)
        for q in range(2):
            sums(q, mine)
        back.wait()
        LOC[:, theirs] = SR[1 + turn]
        for r0 in theirs_at:
            weights(r0)
        ring = {
            (w, c, k): remote(
                RSB.at[turn, i], RRB.at[turn, i], rs_s.at[turn, i], rs_r.at[turn, i], zdev(CHAINS[c][0])
            )
            for (w, c, k), i in MSG.items()
        }

        def ring_hop(w, k, chains=range(4)):
            for c, (d, h, hops) in enumerate(CHAINS):
                if k < hops and c in chains:
                    o = (d * (hops - k)) % NZ
                    v = SUMS[pl.ds(SLOT[o] * CHUNK + (2 * w + h) * PIECE, PIECE), :]
                    if k:
                        ring[w, c, k - 1].wait_recv()
                        v = v + RRB[turn, MSG[w, c, k - 1]].astype(F32)
                    RSB[turn, MSG[w, c, k]] = v.astype(BF16)
                    ring[w, c, k].start()

        sums(0, theirs, add=True)
        for w in range(WAVES):
            ring_hop(w, 0, (0, 1, 2))
        sums(1, theirs, add=True)
        for w in range(WAVES):
            ring_hop(w, 0, (3,))
        for q in (2, 3):
            sums(q, pl.ds(0, 2 * ROWS))
        MS[turn] = jnp.sum(MACC[...].T, axis=0, keepdims=True)
        masses = [
            remote(MS.at[turn], MR.at[turn, h - 1], m_s.at[turn, h - 1], m_r.at[turn, h - 1], zdev(h))
            for h in range(1, NZ)
        ]
        for c in masses:
            c.start()
        for k in range(1, 4):
            for w in range(WAVES):
                ring_hop(w, k)
        for c in masses:
            c.wait()
        lane = lax.broadcasted_iota(jnp.int32, (CHUNK, 128), 1)
        row = lax.broadcasted_iota(jnp.int32, (CHUNK, 128), 0)
        acc = jnp.zeros((CHUNK, 128), F32)
        for h in range(NZ):
            j = SLOT[h]
            vec = MS[turn] if h == 0 else MR[turn, h - 1]
            vec = vec[:, (j // 2) * 128 : (j // 2 + 1) * 128]
            acc = acc + jnp.where(lane == row + CHUNK * (j % 2), jnp.broadcast_to(vec, (CHUNK, 128)), 0.0)
        inv = 1.0 / (jnp.sum(acc, axis=1, keepdims=True) + 1.0)

        def place(o, piece):
            start = piece * PIECE
            if last:
                return out.at[pl.ds(pl.multiple_of(chunk_row(SLOT[o % NZ]) + start, PIECE), PIECE)]
            return CUR.at[turn + 1, pl.ds(SLOT[o % NZ] * CHUNK + start, PIECE)]

        gather, pairs, keeps = {}, {}, []
        for (w, c, k), i in MSG.items():
            d, h, hops = CHAINS[c]
            piece = 2 * w + h
            src = place(-d * k, piece)
            dst = src if last else place(-d * (k + 1), piece)
            if last and k == 0:
                src = CUR.at[0, pl.ds(piece * PIECE, PIECE)]
            gather[w, c, k] = remote(src, dst, ag_s.at[turn, i], ag_r.at[turn, i], zdev(d))
            if last:
                got = place(-d * (k + 1), 2 * w + h)
                pairs[w, c, k] = remote(got, got, o_s.at[i], o_r.at[i], sib)
        if last:
            for w in range(WAVES):
                start = 2 * w * PIECE
                fresh = CUR.at[0, pl.ds(start, 2 * PIECE)]
                rows = out.at[pl.ds(pl.multiple_of(chunk_row(SLOT[0]) + start, 2 * PIECE), 2 * PIECE)]
                pairs[w] = remote(fresh, rows, o_s.at[NMSG + w], o_r.at[NMSG + w], sib)
                keeps.append(pltpu.make_async_copy(fresh, rows, o_l.at[w]))

        def finish(w):
            for h in range(2):
                piece = 2 * w + h
                rows = pl.ds(SLOT[0] * CHUNK + piece * PIECE, PIECE)
                v = SUMS[rows, :] + CUR[turn, rows, :].astype(F32)
                for c in range(4):
                    if CHAINS[c][1] == h:
                        k = CHAINS[c][2] - 1
                        ring[w, c, k].wait_recv()
                        v = v + RRB[turn, MSG[w, c, k]].astype(F32)
                fresh = (v * inv[piece * PIECE : (piece + 1) * PIECE]).astype(BF16)
                if last:
                    CUR[0, pl.ds(piece * PIECE, PIECE), :] = fresh
                else:
                    CUR[turn + 1, rows, :] = fresh
                for c in range(4):
                    if CHAINS[c][1] == h:
                        gather[w, c, 0].start()
            if last:
                pairs[w].start()
                keeps[w].start()

        def gather_hop(w, k):
            for c, (d, h, hops) in enumerate(CHAINS):
                if k <= hops:
                    gather[w, c, k - 1].wait_recv()
                    if k < hops:
                        gather[w, c, k].start()
                    if last:
                        pairs[w, c, k - 1].start()

        for w in range(WAVES):
            finish(w)
        for k in (1, 2):
            for w in range(WAVES):
                gather_hop(w, k)
        if last:
            for k in (3, 4):
                for w in range(WAVES):
                    gather_hop(w, k)
            row_lse[...] = (SS[turn] * LN2).reshape(ROWS)
        else:
            store_norms(NRM, CUR.at[turn + 1], 1)
            run_scores(own_items(turn + 1, [1], mine_at), {})
            gather_hop(0, 3)
            gather_hop(1, 3)
            run_scores(own_items(turn + 1, [1], theirs_at), {})
            gather_hop(0, 4)
            gather_hop(1, 4)
            store_norms(NRM, CUR.at[turn + 1], 0)
        for key in MSG:
            ring[key].wait_send()
            gather[key].wait_send()

    for c in list(pairs.values()) + keeps:
        c.wait()


def per_device(embeds, centroids):
    dma = pltpu.SemaphoreType.DMA
    new, lse = pl.pallas_call(
        kernel,
        out_shape=(
            jax.ShapeDtypeStruct((CENTS, D), BF16),
            jax.ShapeDtypeStruct((ROWS,), F32),
        ),
        in_specs=[pl.BlockSpec(memory_space=pltpu.HBM)] * 2,
        out_specs=(pl.BlockSpec(memory_space=pl.ANY), pl.BlockSpec(memory_space=pltpu.VMEM)),
        scratch_shapes=[
            pltpu.VMEM((2 * ROWS, D), BF16),
            pltpu.VMEM((ITERS, OWN, D), BF16),
            pltpu.VMEM((OWN, D), BF16),
            pltpu.VMEM((OWN, 128), F32),
            pltpu.VMEM((OWN, 128), F32),
            pltpu.VMEM((OWN, 2 * ROWS), F32),
            pltpu.VMEM((OWN, 2 * ROWS), BF16),
            pltpu.VMEM((OWN, D), F32),
            pltpu.VMEM((2, GROUP, RB), F32),
            pltpu.VMEM((2, 1, 2 * ROWS), F32),
            pltpu.VMEM((4, 1, 2 * ROWS), F32),
            pltpu.VMEM((1, 2 * ROWS), F32),
            pltpu.VMEM((ITERS, 1, ROWS), F32),
            pltpu.VMEM((ITERS, NC - 1, 1, ROWS), F32),
            pltpu.VMEM((ITERS, 1, ROWS), F32),
            pltpu.VMEM((ITERS + 1, 1, ROWS), F32),
            pltpu.VMEM((OWN, 128), F32),
            pltpu.VMEM((ITERS, 1, OWN), F32),
            pltpu.VMEM((ITERS, NZ - 1, 1, OWN), F32),
            pltpu.VMEM((ITERS, NMSG, PIECE, D), BF16),
            pltpu.VMEM((ITERS, NMSG, PIECE, D), BF16),
            dma((ROWS // RB,)),
            dma((NZ + 1,)),
            dma((ROWS // RB,)),
            dma((ROWS // RB,)),
            dma((ITERS, NC - 1)),
            dma((ITERS, NC - 1)),
            dma((ITERS + 1,)),
            dma((ITERS + 1,)),
            dma((ITERS, NZ - 1)),
            dma((ITERS, NZ - 1)),
            dma((ITERS, NMSG)),
            dma((ITERS, NMSG)),
            dma((ITERS, NMSG)),
            dma((ITERS, NMSG)),
            dma((WAVES,)),
            dma((NMSG + WAVES,)),
            dma((NMSG + WAVES,)),
        ],
        compiler_params=pltpu.CompilerParams(
            collective_id=0, has_side_effects=True, vmem_limit_bytes=50 * 1024 * 1024
        ),
    )(embeds, centroids)
    return new, lse


def solution(mesh):
    return jax.shard_map(
        per_device,
        mesh=mesh,
        in_specs=(P("dp", None), P("cent", None)),
        out_specs=(P("cent", None), P("dp")),
        check_vma=False,
    )
```

```python
import functools
import math

import jax
import jax.numpy as jnp
from jax import lax
from jax.experimental import pallas as pl
from jax.experimental.pallas import tpu as pltpu
from jax.sharding import PartitionSpec as P

ITERS = 2
TEMP = 2.5
D = 1024
ROWS = 1536
CENTS = 1024
NZ = 8
NC = 16
OWN = CENTS // 2
CHUNK = OWN // NZ
WAVES = 2
PIECE = CHUNK // WAVES // 2
GROUP = OWN // 2
RB = 768
NB = ROWS // RB
KEXP = TEMP * math.log2(math.e)
LN2 = math.log(2.0)

OFF = (4, 3, 5, 2, 6, 1, 7, 0)
SLOT = {o: j for j, o in enumerate(OFF)}
CHAINS = ((1, 0, 4), (-1, 1, 4), (1, 1, 3), (-1, 0, 3))
MSG = {}
for _w in range(WAVES):
    for _c, (_d, _h, _l) in enumerate(CHAINS):
        for _k in range(_l):
            MSG[(_w, _c, _k)] = len(MSG)
NMSG = len(MSG)
NX = NY = 4
PEERS = [(dx, dy) for dx in range(NX) for dy in range(NY) if dx or dy]
PEERS.sort(key=lambda p: -min(p[0], NX - p[0]) - min(p[1], NY - p[1]))
ALONG = sorted(range(1, NZ), key=lambda h: -min(h, NZ - h))
MESH = pl.DeviceIdType.MESH
F32 = jnp.float32
BF16 = jnp.bfloat16


def nt_dot(a, b):
    return lax.dot_general(a, b, (((1,), (1,)), ((), ())), preferred_element_type=F32)


def lse2(parts):
    top = functools.reduce(jnp.maximum, parts)
    return top + jnp.log2(sum(jnp.exp2(p - top) for p in parts))


def kernel(
    emb, cen, out, row_lse,
    E, CUR, CO, NRM, NRO, PB, W, SUMS, SB, MG, LG, LOC, XS, XR, SS, SR, MACC, MS, MR, RSB, RRB,
    ld_e, ld_c, es_s, es_r, x_s, x_r, s_s, s_r, m_s, m_r, rs_s, rs_r, ag_s, ag_r, o_l, o_s, o_r,
):
    dp = lax.axis_index("dp")
    cent = lax.axis_index("cent")
    z = dp // 2
    core = dp % 2
    sib = (z * 2 + (1 - core), cent)

    def zdev(h):
        return (((z + h + NZ) % NZ) * 2 + core, cent)

    def cdev(k):
        dx, dy = PEERS[k]
        return (dp, ((cent // NY + dx) % NX) * NY + (cent % NY + dy) % NY)

    def remote(src, dst, s, r, dev):
        return pltpu.make_async_remote_copy(
            src_ref=src, dst_ref=dst, send_sem=s, recv_sem=r, device_id=dev, device_id_type=MESH
        )

    def chunk_row(j):
        return pl.multiple_of(core * OWN + ((z + OFF[j]) % NZ) * CHUNK, CHUNK)

    barrier = pltpu.get_barrier_semaphore()
    pl.semaphore_signal(barrier, inc=1, device_id=sib, device_id_type=MESH)
    for k in range(NC - 1):
        pl.semaphore_signal(barrier, inc=1, device_id=cdev(k), device_id_type=MESH)
    for h in ALONG:
        pl.semaphore_signal(barrier, inc=1, device_id=zdev(h), device_id_type=MESH)

    load_c = [
        pltpu.make_async_copy(cen.at[pl.ds(chunk_row(j), CHUNK)], CUR.at[0, pl.ds(j * CHUNK, CHUNK)], ld_c.at[j])
        for j in range(NZ)
    ]
    load_c.append(
        pltpu.make_async_copy(cen.at[pl.ds(pl.multiple_of((1 - core) * OWN, OWN), OWN)], CO, ld_c.at[NZ])
    )
    load_e = [
        pltpu.make_async_copy(emb.at[pl.ds(b * RB, RB)], E.at[pl.ds(b * RB, RB)], ld_e.at[b]) for b in range(NB)
    ]
    for c in load_c[:NZ]:
        c.start()
    load_e[0].start()
    load_c[NZ].start()
    for c in load_e[1:]:
        c.start()
    send_e = [
        remote(emb.at[pl.ds(b * RB, RB)], E.at[pl.ds(ROWS + b * RB, RB)], es_s.at[b], es_r.at[b], sib)
        for b in range(NB)
    ]

    def meet():
        pl.semaphore_wait(barrier, NC - 1 + NZ - 1 + 1)
        for c in send_e:
            c.start()

    def store_norms(dst, src, g):
        rows = pl.ds(g * GROUP, GROUP)
        n = (0.5 * KEXP) * jnp.sum(jnp.square(src[rows, :].astype(F32)), axis=1, keepdims=True)
        dst[rows, :] = jnp.broadcast_to(n, (GROUP, 128))

    def run_scores(items, hooks):
        def product(i):
            if i in hooks:
                hooks[i]()
            c, _, g, r0, _, _ = items[i]
            SB[i % 2] = nt_dot(c[pl.ds(g * GROUP, GROUP), :], E[pl.ds(r0, RB), :])

        product(0)
        for i, (_, norms, g, r0, slot, keep) in enumerate(items):
            if i + 1 < len(items):
                product(i + 1)
            rows, cols = pl.ds(g * GROUP, GROUP), pl.ds(r0, RB)
            s = KEXP * SB[i % 2] - jnp.concatenate([norms[rows, :]] * (RB // 128), axis=1)
            m = jnp.max(s, axis=0, keepdims=True)
            p = jnp.exp2(s - m)
            LG[slot, :, cols] = m + jnp.log2(jnp.sum(p, axis=0, keepdims=True))
            if keep:
                PB[rows, cols] = p
                MG[g, :, cols] = m

    def own_items(turn, groups, starts):
        return [(CUR.at[turn], NRM, g, r0, g, True) for r0 in starts for g in groups]

    mine_at, theirs_at = range(0, ROWS, RB), range(ROWS, 2 * ROWS, RB)
    meet()
    for c in load_c:
        c.wait()
    for g in range(2):
        store_norms(NRM, CUR.at[0], g)
        store_norms(NRO, CO, g)
    load_e[0].wait()
    mine, theirs = pl.ds(0, ROWS), pl.ds(ROWS, ROWS)

    late = []
    for turn in range(ITERS):
        last = turn == ITERS - 1
        if turn == 0:
            items = []
            for r0 in mine_at:
                items += own_items(0, range(2), [r0])
                items += [(CO, NRO, g, r0, 2 + g, False) for g in range(2)]
            run_scores(items, {4: load_e[1].wait})
            XS[turn] = lse2([LG[i, :, mine] for i in range(4)])
        else:
            run_scores(own_items(turn, [0], theirs_at), {})
            LOC[:, theirs] = lse2([LG[0, :, theirs], LG[1, :, theirs]])
            part = remote(LOC.at[:, theirs], SR.at[0], s_s.at[0], s_r.at[0], sib)
            part.start()
            run_scores(own_items(turn, [0], mine_at), {})
            both = lse2([LG[0, :, mine], LG[1, :, mine]])
            part.wait()
            XS[turn] = lse2([both, SR[0]])

        sends = [
            remote(XS.at[turn], XR.at[turn, k], x_s.at[turn], x_r.at[turn], cdev(k)) for k in range(NC - 1)
        ]
        for c in sends:
            c.start()
        if turn == 0:
            send_e[0].wait_recv()
            run_scores(own_items(0, range(2), theirs_at), {2: send_e[1].wait_recv})

        late.append(remote(XR.at[turn], XR.at[turn], x_s.at[turn], x_r.at[turn], sib))
        late[-1].wait_recv()
        total = lse2([XS[turn]] + [XR[turn, k] for k in range(NC - 1)])
        SS[turn] = total
        LOC[:, mine] = total
        back = remote(SS.at[turn], SR.at[1 + turn], s_s.at[1 + turn], s_r.at[1 + turn], sib)
        back.start()
        MACC[...] = jnp.zeros_like(MACC)

        def weights(r0):
            lse = LOC[:, pl.ds(r0, RB)]
            for g in range(2):
                rows = pl.ds(g * GROUP, GROUP)
                w = (PB[rows, pl.ds(r0, RB)] * jnp.exp2(MG[g, :, pl.ds(r0, RB)] - lse)).astype(BF16)
                W[rows, pl.ds(r0, RB)] = w
                wf = w.astype(F32)
                MACC[rows, :] += sum(wf[:, i * 128 : (i + 1) * 128] for i in range(RB // 128))

        def sums(q, depth, add=False):
            rows = pl.ds(q * 2 * CHUNK, 2 * CHUNK)
            v = jnp.dot(W[rows, depth], E[depth, :], preferred_element_type=F32)
            SUMS[rows, :] = SUMS[rows, :] + v if add else v

        for r0 in mine_at:
            weights(r0)
        for q in range(2):
            sums(q, mine)
        back.wait()
        LOC[:, theirs] = SR[1 + turn]
        for r0 in theirs_at:
            weights(r0)
        ring = {
            (w, c, k): remote(
                RSB.at[turn, i], RRB.at[turn, i], rs_s.at[turn], rs_r.at[turn, i], zdev(CHAINS[c][0])
            )
            for (w, c, k), i in MSG.items()
        }

        def ring_hop(w, k, chains=range(4)):
            for c, (d, h, hops) in enumerate(CHAINS):
                if k < hops and c in chains:
                    o = (d * (hops - k)) % NZ
                    v = SUMS[pl.ds(SLOT[o] * CHUNK + (2 * w + h) * PIECE, PIECE), :]
                    if k:
                        ring[w, c, k - 1].wait_recv()
                        v = v + RRB[turn, MSG[w, c, k - 1]].astype(F32)
                    RSB[turn, MSG[w, c, k]] = v.astype(BF16)
                    ring[w, c, k].start()

        sums(0, theirs, add=True)
        for w in range(WAVES):
            ring_hop(w, 0, (0, 1, 2))
        sums(1, theirs, add=True)
        for w in range(WAVES):
            ring_hop(w, 0, (3,))
        for q in (2, 3):
            sums(q, pl.ds(0, 2 * ROWS))
        MS[turn] = jnp.sum(MACC[...].T, axis=0, keepdims=True)
        masses = [
            remote(MS.at[turn], MR.at[turn, h - 1], m_s.at[turn], m_r.at[turn], zdev(h)) for h in ALONG
        ]
        for c in masses:
            c.start()
        for k in range(1, 4):
            for w in range(WAVES):
                ring_hop(w, k)
        late.append(remote(MR.at[turn], MR.at[turn], m_s.at[turn], m_r.at[turn], sib))
        late[-1].wait_recv()
        lane = lax.broadcasted_iota(jnp.int32, (CHUNK, 128), 1)
        row = lax.broadcasted_iota(jnp.int32, (CHUNK, 128), 0)
        acc = jnp.zeros((CHUNK, 128), F32)
        for h in range(NZ):
            j = SLOT[h]
            vec = MS[turn] if h == 0 else MR[turn, h - 1]
            vec = vec[:, (j // 2) * 128 : (j // 2 + 1) * 128]
            acc = acc + jnp.where(lane == row + CHUNK * (j % 2), jnp.broadcast_to(vec, (CHUNK, 128)), 0.0)
        inv = 1.0 / (jnp.sum(acc, axis=1, keepdims=True) + 1.0)

        def place(o, piece):
            start = piece * PIECE
            if last:
                return out.at[pl.ds(pl.multiple_of(chunk_row(SLOT[o % NZ]) + start, PIECE), PIECE)]
            return CUR.at[turn + 1, pl.ds(SLOT[o % NZ] * CHUNK + start, PIECE)]

        gather, pairs, keeps = {}, {}, []
        for (w, c, k), i in MSG.items():
            d, h, hops = CHAINS[c]
            piece = 2 * w + h
            src = place(-d * k, piece)
            dst = src if last else place(-d * (k + 1), piece)
            if last and k == 0:
                src = CUR.at[0, pl.ds(piece * PIECE, PIECE)]
            gather[w, c, k] = remote(src, dst, ag_s.at[turn], ag_r.at[turn, i], zdev(d))
            if last:
                got = place(-d * (k + 1), 2 * w + h)
                pairs[w, c, k] = remote(got, got, o_s.at[0], o_r.at[0], sib)
        if last:
            for w in range(WAVES):
                start = 2 * w * PIECE
                fresh = CUR.at[0, pl.ds(start, 2 * PIECE)]
                rows = out.at[pl.ds(pl.multiple_of(chunk_row(SLOT[0]) + start, 2 * PIECE), 2 * PIECE)]
                pairs[w] = remote(fresh, rows, o_s.at[0], o_r.at[0], sib)
                keeps.append(pltpu.make_async_copy(fresh, rows, o_l.at[w]))

        def finish(w):
            for h in range(2):
                piece = 2 * w + h
                rows = pl.ds(SLOT[0] * CHUNK + piece * PIECE, PIECE)
                v = SUMS[rows, :] + CUR[turn, rows, :].astype(F32)
                for c in range(4):
                    if CHAINS[c][1] == h:
                        k = CHAINS[c][2] - 1
                        ring[w, c, k].wait_recv()
                        v = v + RRB[turn, MSG[w, c, k]].astype(F32)
                fresh = (v * inv[piece * PIECE : (piece + 1) * PIECE]).astype(BF16)
                if last:
                    CUR[0, pl.ds(piece * PIECE, PIECE), :] = fresh
                else:
                    CUR[turn + 1, rows, :] = fresh
                for c in range(4):
                    if CHAINS[c][1] == h:
                        gather[w, c, 0].start()
            if last:
                pairs[w].start()
                keeps[w].start()

        def gather_hop(w, k):
            for c, (d, h, hops) in enumerate(CHAINS):
                if k <= hops:
                    gather[w, c, k - 1].wait_recv()
                    if k < hops:
                        gather[w, c, k].start()
                    if last:
                        pairs[w, c, k - 1].start()

        for w in range(WAVES):
            finish(w)
        for k in (1, 2):
            for w in range(WAVES):
                gather_hop(w, k)
        if last:
            for k in (3, 4):
                for w in range(WAVES):
                    gather_hop(w, k)
            row_lse[...] = (SS[turn] * LN2).reshape(ROWS)
        else:
            store_norms(NRM, CUR.at[turn + 1], 1)
            run_scores(own_items(turn + 1, [1], mine_at), {})
            gather_hop(0, 3)
            gather_hop(1, 3)
            run_scores(own_items(turn + 1, [1], theirs_at), {})
            gather_hop(0, 4)
            gather_hop(1, 4)
            store_norms(NRM, CUR.at[turn + 1], 0)
        late.append(remote(RSB.at[turn], RSB.at[turn], rs_s.at[turn], rs_r.at[turn, 0], sib))
        late.append(remote(RSB.at[turn], RSB.at[turn], ag_s.at[turn], ag_r.at[turn, 0], sib))

    for c in late + send_e:
        c.wait_send()
    for c in keeps:
        c.wait()
    remote(CUR.at[1], CUR.at[1], o_s.at[0], o_r.at[0], sib).wait()


def per_device(embeds, centroids):
    dma = pltpu.SemaphoreType.DMA
    new, lse = pl.pallas_call(
        kernel,
        out_shape=(
            jax.ShapeDtypeStruct((CENTS, D), BF16),
            jax.ShapeDtypeStruct((ROWS,), F32),
        ),
        in_specs=[pl.BlockSpec(memory_space=pltpu.HBM)] * 2,
        out_specs=(pl.BlockSpec(memory_space=pl.ANY), pl.BlockSpec(memory_space=pltpu.VMEM)),
        scratch_shapes=[
            pltpu.VMEM((2 * ROWS, D), BF16),
            pltpu.VMEM((ITERS, OWN, D), BF16),
            pltpu.VMEM((OWN, D), BF16),
            pltpu.VMEM((OWN, 128), F32),
            pltpu.VMEM((OWN, 128), F32),
            pltpu.VMEM((OWN, 2 * ROWS), F32),
            pltpu.VMEM((OWN, 2 * ROWS), BF16),
            pltpu.VMEM((OWN, D), F32),
            pltpu.VMEM((2, GROUP, RB), F32),
            pltpu.VMEM((2, 1, 2 * ROWS), F32),
            pltpu.VMEM((4, 1, 2 * ROWS), F32),
            pltpu.VMEM((1, 2 * ROWS), F32),
            pltpu.VMEM((ITERS, 1, ROWS), F32),
            pltpu.VMEM((ITERS, NC - 1, 1, ROWS), F32),
            pltpu.VMEM((ITERS, 1, ROWS), F32),
            pltpu.VMEM((ITERS + 1, 1, ROWS), F32),
            pltpu.VMEM((OWN, 128), F32),
            pltpu.VMEM((ITERS, 1, OWN), F32),
            pltpu.VMEM((ITERS, NZ - 1, 1, OWN), F32),
            pltpu.VMEM((ITERS, NMSG, PIECE, D), BF16),
            pltpu.VMEM((ITERS, NMSG, PIECE, D), BF16),
            dma((ROWS // RB,)),
            dma((NZ + 1,)),
            dma((ROWS // RB,)),
            dma((ROWS // RB,)),
            dma((ITERS,)),
            dma((ITERS,)),
            dma((ITERS + 1,)),
            dma((ITERS + 1,)),
            dma((ITERS,)),
            dma((ITERS,)),
            dma((ITERS,)),
            dma((ITERS, NMSG)),
            dma((ITERS,)),
            dma((ITERS, NMSG)),
            dma((WAVES,)),
            dma((1,)),
            dma((1,)),
        ],
        compiler_params=pltpu.CompilerParams(
            collective_id=0, has_side_effects=True, vmem_limit_bytes=50 * 1024 * 1024
        ),
    )(embeds, centroids)
    return new, lse


def solution(mesh):
    return jax.shard_map(
        per_device,
        mesh=mesh,
        in_specs=(P("dp", None), P("cent", None)),
        out_specs=(P("cent", None), P("dp")),
        check_vma=False,
    )
```

```python
import functools
import math

import jax
import jax.numpy as jnp
from jax import lax
from jax.experimental import pallas as pl
from jax.experimental.pallas import tpu as pltpu
from jax.sharding import PartitionSpec as P

ITERS = 2
TEMP = 2.5
D = 1024
ROWS = 1536
CENTS = 1024
NZ = 8
NC = 16
OWN = CENTS // 2
CHUNK = OWN // NZ
WAVES = 2
PIECE = CHUNK // WAVES // 2
GROUP = OWN // 2
RB = 768
NB = ROWS // RB
KEXP = TEMP * math.log2(math.e)
LN2 = math.log(2.0)

OFF = (4, 3, 5, 2, 6, 1, 7, 0)
SLOT = {o: j for j, o in enumerate(OFF)}
CHAINS = ((1, 0, 4), (-1, 1, 4), (1, 1, 3), (-1, 0, 3))
MSG = {}
for _w in range(WAVES):
    for _c, (_d, _h, _l) in enumerate(CHAINS):
        for _k in range(_l):
            MSG[(_w, _c, _k)] = len(MSG)
NMSG = len(MSG)
NX = NY = 4
PEERS = [(dx, dy) for dx in range(NX) for dy in range(NY) if dx or dy]
PEERS.sort(key=lambda p: -min(p[0], NX - p[0]) - min(p[1], NY - p[1]))
ALONG = sorted(range(1, NZ), key=lambda h: -min(h, NZ - h))
LINKS = {4: (1, 2, 1, 1), 3: (1, 1, 1)}
SUMMED = {4: (4, 3, 1, 2), 3: (3, 2, 1)}
ADDS = {4: ((), (0,), (1, 3), ()), 3: ((), (0,), (1,))}
HELD = {4: (0, 1, 3, 1), 3: (0, 1, 2)}
MESH = pl.DeviceIdType.MESH
F32 = jnp.float32
BF16 = jnp.bfloat16


def nt_dot(a, b):
    return lax.dot_general(a, b, (((1,), (1,)), ((), ())), preferred_element_type=F32)


def lse2(parts):
    top = functools.reduce(jnp.maximum, parts)
    return top + jnp.log2(sum(jnp.exp2(p - top) for p in parts))


def kernel(
    emb, cen, out, row_lse,
    E, CUR, CO, NRM, NRO, PB, W, SUMS, SB, MG, LG, LOC, XS, XR, SS, SR, MACC, MS, MR, RSB, RRB,
    ld_e, ld_c, es_s, es_r, x_s, x_r, s_s, s_r, m_s, m_r, rs_s, rs_r, ag_s, ag_r, o_l, o_s, o_r,
):
    dp = lax.axis_index("dp")
    cent = lax.axis_index("cent")
    z = dp // 2
    core = dp % 2
    sib = (z * 2 + (1 - core), cent)

    def zdev(h):
        return (((z + h + NZ) % NZ) * 2 + core, cent)

    def cdev(k):
        dx, dy = PEERS[k]
        return (dp, ((cent // NY + dx) % NX) * NY + (cent % NY + dy) % NY)

    def remote(src, dst, s, r, dev):
        return pltpu.make_async_remote_copy(
            src_ref=src, dst_ref=dst, send_sem=s, recv_sem=r, device_id=dev, device_id_type=MESH
        )

    def chunk_row(j):
        return pl.multiple_of(core * OWN + ((z + OFF[j]) % NZ) * CHUNK, CHUNK)

    barrier = pltpu.get_barrier_semaphore()
    pl.semaphore_signal(barrier, inc=1, device_id=sib, device_id_type=MESH)
    for k in range(NC - 1):
        pl.semaphore_signal(barrier, inc=1, device_id=cdev(k), device_id_type=MESH)
    for h in ALONG:
        pl.semaphore_signal(barrier, inc=1, device_id=zdev(h), device_id_type=MESH)

    load_c = [
        pltpu.make_async_copy(cen.at[pl.ds(chunk_row(j), CHUNK)], CUR.at[0, pl.ds(j * CHUNK, CHUNK)], ld_c.at[j])
        for j in range(NZ)
    ]
    load_c.append(
        pltpu.make_async_copy(cen.at[pl.ds(pl.multiple_of((1 - core) * OWN, OWN), OWN)], CO, ld_c.at[NZ])
    )
    load_e = [
        pltpu.make_async_copy(emb.at[pl.ds(b * RB, RB)], E.at[pl.ds(b * RB, RB)], ld_e.at[b]) for b in range(NB)
    ]
    for c in load_c[:NZ]:
        c.start()
    load_e[0].start()
    load_c[NZ].start()
    for c in load_e[1:]:
        c.start()
    send_e = [
        remote(emb.at[pl.ds(b * RB, RB)], E.at[pl.ds(ROWS + b * RB, RB)], es_s.at[b], es_r.at[b], sib)
        for b in range(NB)
    ]

    def meet():
        pl.semaphore_wait(barrier, NC - 1 + NZ - 1 + 1)
        for c in send_e:
            c.start()

    def store_norms(dst, src, g):
        rows = pl.ds(g * GROUP, GROUP)
        n = (0.5 * KEXP) * jnp.sum(jnp.square(src[rows, :].astype(F32)), axis=1, keepdims=True)
        dst[rows, :] = jnp.broadcast_to(n, (GROUP, 128))

    def run_scores(items, hooks):
        def product(i):
            if i in hooks:
                hooks[i]()
            c, _, g, r0, _, _ = items[i]
            SB[i % 2] = nt_dot(c[pl.ds(g * GROUP, GROUP), :], E[pl.ds(r0, RB), :])

        product(0)
        for i, (_, norms, g, r0, slot, keep) in enumerate(items):
            if i + 1 < len(items):
                product(i + 1)
            rows, cols = pl.ds(g * GROUP, GROUP), pl.ds(r0, RB)
            s = KEXP * SB[i % 2] - jnp.concatenate([norms[rows, :]] * (RB // 128), axis=1)
            m = jnp.max(s, axis=0, keepdims=True)
            p = jnp.exp2(s - m)
            LG[slot, :, cols] = m + jnp.log2(jnp.sum(p, axis=0, keepdims=True))
            if keep:
                PB[rows, cols] = p
                MG[g, :, cols] = m

    def own_items(turn, groups, starts):
        return [(CUR.at[turn], NRM, g, r0, g, True) for r0 in starts for g in groups]

    mine_at, theirs_at = range(0, ROWS, RB), range(ROWS, 2 * ROWS, RB)
    meet()
    for c in load_c:
        c.wait()
    for g in range(2):
        store_norms(NRM, CUR.at[0], g)
        store_norms(NRO, CO, g)
    load_e[0].wait()
    mine, theirs = pl.ds(0, ROWS), pl.ds(ROWS, ROWS)

    late = []
    for turn in range(ITERS):
        last = turn == ITERS - 1
        if turn == 0:
            items = []
            for r0 in mine_at:
                items += own_items(0, range(2), [r0])
                items += [(CO, NRO, g, r0, 2 + g, False) for g in range(2)]
            run_scores(items, {4: load_e[1].wait})
            XS[turn] = lse2([LG[i, :, mine] for i in range(4)])
        else:
            run_scores(own_items(turn, [0], theirs_at), {})
            LOC[:, theirs] = lse2([LG[0, :, theirs], LG[1, :, theirs]])
            part = remote(LOC.at[:, theirs], SR.at[0], s_s.at[0], s_r.at[0], sib)
            part.start()
            run_scores(own_items(turn, [0], mine_at), {})
            both = lse2([LG[0, :, mine], LG[1, :, mine]])
            part.wait()
            XS[turn] = lse2([both, SR[0]])

        sends = [
            remote(XS.at[turn], XR.at[turn, k], x_s.at[turn], x_r.at[turn], cdev(k)) for k in range(NC - 1)
        ]
        for c in sends:
            c.start()
        if turn == 0:
            send_e[0].wait_recv()
            run_scores(own_items(0, range(2), theirs_at), {2: send_e[1].wait_recv})

        late.append(remote(XR.at[turn], XR.at[turn], x_s.at[turn], x_r.at[turn], sib))
        late[-1].wait_recv()
        total = lse2([XS[turn]] + [XR[turn, k] for k in range(NC - 1)])
        SS[turn] = total
        LOC[:, mine] = total
        back = remote(SS.at[turn], SR.at[1 + turn], s_s.at[1 + turn], s_r.at[1 + turn], sib)
        back.start()
        MACC[...] = jnp.zeros_like(MACC)

        def weights(r0):
            lse = LOC[:, pl.ds(r0, RB)]
            for g in range(2):
                rows = pl.ds(g * GROUP, GROUP)
                w = (PB[rows, pl.ds(r0, RB)] * jnp.exp2(MG[g, :, pl.ds(r0, RB)] - lse)).astype(BF16)
                W[rows, pl.ds(r0, RB)] = w
                wf = w.astype(F32)
                MACC[rows, :] += sum(wf[:, i * 128 : (i + 1) * 128] for i in range(RB // 128))

        def sums(q, depth, add=False):
            rows = pl.ds(q * 2 * CHUNK, 2 * CHUNK)
            v = jnp.dot(W[rows, depth], E[depth, :], preferred_element_type=F32)
            SUMS[rows, :] = SUMS[rows, :] + v if add else v

        for r0 in mine_at:
            weights(r0)
        for q in range(2):
            sums(q, mine)
        back.wait()
        LOC[:, theirs] = SR[1 + turn]
        for r0 in theirs_at:
            weights(r0)
        ring = {
            (w, c, k): remote(
                RSB.at[turn, i], RRB.at[turn, i], rs_s.at[turn], rs_r.at[turn, i],
                zdev(CHAINS[c][0] * LINKS[CHAINS[c][2]][k]),
            )
            for (w, c, k), i in MSG.items()
        }

        def ring_send(k, chains):
            for w in range(WAVES):
                for c in chains:
                    d, h, reach = CHAINS[c]
                    o = (d * SUMMED[reach][k]) % NZ
                    v = SUMS[pl.ds(SLOT[o] * CHUNK + (2 * w + h) * PIECE, PIECE), :]
                    for j in ADDS[reach][k]:
                        ring[w, c, j].wait_recv()
                        v = v + RRB[turn, MSG[w, c, j]].astype(F32)
                    RSB[turn, MSG[w, c, k]] = v.astype(BF16)
                    ring[w, c, k].start()

        sums(0, theirs, add=True)
        ring_send(0, (0, 1, 2))
        sums(1, theirs, add=True)
        ring_send(0, (3,))
        ring_send(3, (0,))
        sums(2, pl.ds(0, 2 * ROWS))
        ring_send(3, (1,))
        sums(3, pl.ds(0, 2 * ROWS))
        MS[turn] = jnp.sum(MACC[...].T, axis=0, keepdims=True)
        masses = [
            remote(MS.at[turn], MR.at[turn, h - 1], m_s.at[turn], m_r.at[turn], zdev(h)) for h in ALONG
        ]
        for c in masses:
            c.start()
        for k in (1, 2):
            ring_send(k, range(4))
        late.append(remote(MR.at[turn], MR.at[turn], m_s.at[turn], m_r.at[turn], sib))
        late[-1].wait_recv()
        lane = lax.broadcasted_iota(jnp.int32, (CHUNK, 128), 1)
        row = lax.broadcasted_iota(jnp.int32, (CHUNK, 128), 0)
        acc = jnp.zeros((CHUNK, 128), F32)
        for h in range(NZ):
            j = SLOT[h]
            vec = MS[turn] if h == 0 else MR[turn, h - 1]
            vec = vec[:, (j // 2) * 128 : (j // 2 + 1) * 128]
            acc = acc + jnp.where(lane == row + CHUNK * (j % 2), jnp.broadcast_to(vec, (CHUNK, 128)), 0.0)
        inv = 1.0 / (jnp.sum(acc, axis=1, keepdims=True) + 1.0)

        def place(o, piece):
            start = piece * PIECE
            if last:
                return out.at[pl.ds(pl.multiple_of(chunk_row(SLOT[o % NZ]) + start, PIECE), PIECE)]
            return CUR.at[turn + 1, pl.ds(SLOT[o % NZ] * CHUNK + start, PIECE)]

        gather, pairs, keeps = {}, {}, []
        for (w, c, k), i in MSG.items():
            d, h, reach = CHAINS[c]
            piece = 2 * w + h
            held, links = HELD[reach][k], LINKS[reach][k]
            src = place(-d * held, piece)
            dst = src if last else place(-d * (held + links), piece)
            if last and k == 0:
                src = CUR.at[0, pl.ds(piece * PIECE, PIECE)]
            gather[w, c, k] = remote(src, dst, ag_s.at[turn], ag_r.at[turn, i], zdev(d * links))
            if last:
                got = place(-d * (held + links), piece)
                pairs[w, c, k] = remote(got, got, o_s.at[0], o_r.at[0], sib)
        if last:
            for w in range(WAVES):
                start = 2 * w * PIECE
                fresh = CUR.at[0, pl.ds(start, 2 * PIECE)]
                rows = out.at[pl.ds(pl.multiple_of(chunk_row(SLOT[0]) + start, 2 * PIECE), 2 * PIECE)]
                pairs[w] = remote(fresh, rows, o_s.at[0], o_r.at[0], sib)
                keeps.append(pltpu.make_async_copy(fresh, rows, o_l.at[w]))

        def finish(w):
            for h in range(2):
                piece = 2 * w + h
                rows = pl.ds(SLOT[0] * CHUNK + piece * PIECE, PIECE)
                v = SUMS[rows, :] + CUR[turn, rows, :].astype(F32)
                for c in range(4):
                    if CHAINS[c][1] == h:
                        ring[w, c, 2].wait_recv()
                        v = v + RRB[turn, MSG[w, c, 2]].astype(F32)
                fresh = (v * inv[piece * PIECE : (piece + 1) * PIECE]).astype(BF16)
                if last:
                    CUR[0, pl.ds(piece * PIECE, PIECE), :] = fresh
                else:
                    CUR[turn + 1, rows, :] = fresh
                for c in range(4):
                    if CHAINS[c][1] == h:
                        gather[w, c, 0].start()
            if last:
                pairs[w].start()
                keeps[w].start()

        def gather_stage(stage):
            for w in range(WAVES):
                for c, (d, h, reach) in enumerate(CHAINS):
                    gather[w, c, stage - 1].wait_recv()
                    if stage < 3:
                        gather[w, c, stage].start()
                    if stage == 1 and reach == 4:
                        gather[w, c, 3].start()
                    if last:
                        pairs[w, c, stage - 1].start()
            if stage == 2:
                for w in range(WAVES):
                    for c in (0, 1):
                        gather[w, c, 3].wait_recv()
                        if last:
                            pairs[w, c, 3].start()

        for w in range(WAVES):
            finish(w)
        gather_stage(1)
        gather_stage(2)
        if last:
            gather_stage(3)
            row_lse[...] = (SS[turn] * LN2).reshape(ROWS)
        else:
            store_norms(NRM, CUR.at[turn + 1], 1)
            run_scores(own_items(turn + 1, [1], mine_at), {})
            run_scores(own_items(turn + 1, [1], theirs_at), {})
            gather_stage(3)
            store_norms(NRM, CUR.at[turn + 1], 0)
        late.append(remote(RSB.at[turn], RSB.at[turn], rs_s.at[turn], rs_r.at[turn, 0], sib))
        late.append(remote(RSB.at[turn], RSB.at[turn], ag_s.at[turn], ag_r.at[turn, 0], sib))

    for c in late + send_e:
        c.wait_send()
    for c in keeps:
        c.wait()
    remote(CUR.at[1], CUR.at[1], o_s.at[0], o_r.at[0], sib).wait()


def per_device(embeds, centroids):
    dma = pltpu.SemaphoreType.DMA
    new, lse = pl.pallas_call(
        kernel,
        out_shape=(
            jax.ShapeDtypeStruct((CENTS, D), BF16),
            jax.ShapeDtypeStruct((ROWS,), F32),
        ),
        in_specs=[pl.BlockSpec(memory_space=pltpu.HBM)] * 2,
        out_specs=(pl.BlockSpec(memory_space=pl.ANY), pl.BlockSpec(memory_space=pltpu.VMEM)),
        scratch_shapes=[
            pltpu.VMEM((2 * ROWS, D), BF16),
            pltpu.VMEM((ITERS, OWN, D), BF16),
            pltpu.VMEM((OWN, D), BF16),
            pltpu.VMEM((OWN, 128), F32),
            pltpu.VMEM((OWN, 128), F32),
            pltpu.VMEM((OWN, 2 * ROWS), F32),
            pltpu.VMEM((OWN, 2 * ROWS), BF16),
            pltpu.VMEM((OWN, D), F32),
            pltpu.VMEM((2, GROUP, RB), F32),
            pltpu.VMEM((2, 1, 2 * ROWS), F32),
            pltpu.VMEM((4, 1, 2 * ROWS), F32),
            pltpu.VMEM((1, 2 * ROWS), F32),
            pltpu.VMEM((ITERS, 1, ROWS), F32),
            pltpu.VMEM((ITERS, NC - 1, 1, ROWS), F32),
            pltpu.VMEM((ITERS, 1, ROWS), F32),
            pltpu.VMEM((ITERS + 1, 1, ROWS), F32),
            pltpu.VMEM((OWN, 128), F32),
            pltpu.VMEM((ITERS, 1, OWN), F32),
            pltpu.VMEM((ITERS, NZ - 1, 1, OWN), F32),
            pltpu.VMEM((ITERS, NMSG, PIECE, D), BF16),
            pltpu.VMEM((ITERS, NMSG, PIECE, D), BF16),
            dma((ROWS // RB,)),
            dma((NZ + 1,)),
            dma((ROWS // RB,)),
            dma((ROWS // RB,)),
            dma((ITERS,)),
            dma((ITERS,)),
            dma((ITERS + 1,)),
            dma((ITERS + 1,)),
            dma((ITERS,)),
            dma((ITERS,)),
            dma((ITERS,)),
            dma((ITERS, NMSG)),
            dma((ITERS,)),
            dma((ITERS, NMSG)),
            dma((WAVES,)),
            dma((1,)),
            dma((1,)),
        ],
        compiler_params=pltpu.CompilerParams(
            collective_id=0, has_side_effects=True, vmem_limit_bytes=50 * 1024 * 1024
        ),
    )(embeds, centroids)
    return new, lse


def solution(mesh):
    return jax.shard_map(
        per_device,
        mesh=mesh,
        in_specs=(P("dp", None), P("cent", None)),
        out_specs=(P("cent", None), P("dp")),
        check_vma=False,
    )
```

```python
import functools
import math

import jax
import jax.numpy as jnp
from jax import lax
from jax.experimental import pallas as pl
from jax.experimental.pallas import tpu as pltpu
from jax.sharding import PartitionSpec as P

ITERS = 2
TEMP = 2.5
D = 1024
ROWS = 1536
CENTS = 1024
NZ = 8
NC = 16
OWN = CENTS // 2
CHUNK = OWN // NZ
WAVES = 2
PIECE = CHUNK // WAVES // 2
GROUP = OWN // 2
RB = 768
NB = ROWS // RB
KEXP = TEMP * math.log2(math.e)
LN2 = math.log(2.0)

OFF = (4, 3, 5, 2, 6, 1, 7, 0)
SLOT = {o: j for j, o in enumerate(OFF)}
CHAINS = ((1, 0, 4), (-1, 1, 4), (1, 1, 3), (-1, 0, 3))
MSG = {}
for _w in range(WAVES):
    for _c, (_d, _h, _l) in enumerate(CHAINS):
        for _k in range(_l):
            MSG[(_w, _c, _k)] = len(MSG)
NMSG = len(MSG)
NX = NY = 4
PEERS = [(dx, dy) for dx in range(NX) for dy in range(NY) if dx or dy]
PEERS.sort(key=lambda p: -min(p[0], NX - p[0]) - min(p[1], NY - p[1]))
ALONG = sorted(range(1, NZ), key=lambda h: -min(h, NZ - h))
LINKS = {4: (1, 2, 1, 1), 3: (1, 1, 1)}
SUMMED = {4: (4, 3, 1, 2), 3: (3, 2, 1)}
ADDS = {4: ((), (0,), (1, 3), ()), 3: ((), (0,), (1,))}
HELD = {4: (0, 1, 3, 1), 3: (0, 1, 2)}
MESH = pl.DeviceIdType.MESH
F32 = jnp.float32
BF16 = jnp.bfloat16


def nt_dot(a, b):
    return lax.dot_general(a, b, (((1,), (1,)), ((), ())), preferred_element_type=F32)


def lse2(parts):
    top = functools.reduce(jnp.maximum, parts)
    return top + jnp.log2(sum(jnp.exp2(p - top) for p in parts))


def kernel(
    emb, cen, out, row_lse,
    E, CUR, CO, NRM, NRO, PB, W, SUMS, SB, MG, LG, LOC, XS, XR, SS, SR, MACC, MS, MR, RSB, RRB,
    ld_e, ld_c, es_s, es_r, x_s, x_r, s_s, s_r, m_s, m_r, rs_s, rs_r, ag_s, ag_r, o_l, o_s, o_r,
):
    dp = lax.axis_index("dp")
    cent = lax.axis_index("cent")
    z = dp // 2
    core = dp % 2
    sib = (z * 2 + (1 - core), cent)

    def zdev(h):
        return (((z + h + NZ) % NZ) * 2 + core, cent)

    def cdev(k):
        dx, dy = PEERS[k]
        return (dp, ((cent // NY + dx) % NX) * NY + (cent % NY + dy) % NY)

    def remote(src, dst, s, r, dev):
        return pltpu.make_async_remote_copy(
            src_ref=src, dst_ref=dst, send_sem=s, recv_sem=r, device_id=dev, device_id_type=MESH
        )

    def chunk_row(j):
        return pl.multiple_of(core * OWN + ((z + OFF[j]) % NZ) * CHUNK, CHUNK)

    barrier = pltpu.get_barrier_semaphore()
    pl.semaphore_signal(barrier, inc=1, device_id=sib, device_id_type=MESH)
    for k in range(NC - 1):
        pl.semaphore_signal(barrier, inc=1, device_id=cdev(k), device_id_type=MESH)
    for h in ALONG:
        pl.semaphore_signal(barrier, inc=1, device_id=zdev(h), device_id_type=MESH)

    load_c = [
        pltpu.make_async_copy(cen.at[pl.ds(chunk_row(j), CHUNK)], CUR.at[0, pl.ds(j * CHUNK, CHUNK)], ld_c.at[j])
        for j in range(NZ)
    ]
    load_c.append(
        pltpu.make_async_copy(cen.at[pl.ds(pl.multiple_of((1 - core) * OWN, OWN), OWN)], CO, ld_c.at[NZ])
    )
    load_e = [
        pltpu.make_async_copy(emb.at[pl.ds(b * RB, RB)], E.at[pl.ds(b * RB, RB)], ld_e.at[b]) for b in range(NB)
    ]
    for c in load_e + load_c:
        c.start()
    send_e = [
        remote(E.at[pl.ds(b * RB, RB)], E.at[pl.ds(ROWS + b * RB, RB)], es_s.at[b], es_r.at[b], sib)
        for b in range(NB)
    ]

    def meet():
        pl.semaphore_wait(barrier, NC - 1 + NZ - 1 + 1)
        for load, send in zip(load_e, send_e):
            load.wait()
            send.start()

    def store_norms(dst, src, g):
        rows = pl.ds(g * GROUP, GROUP)
        n = (0.5 * KEXP) * jnp.sum(jnp.square(src[rows, :].astype(F32)), axis=1, keepdims=True)
        dst[rows, :] = jnp.broadcast_to(n, (GROUP, 128))

    def run_scores(items, hooks):
        def product(i):
            if i in hooks:
                hooks[i]()
            c, _, g, r0, _, _ = items[i]
            SB[i % 2] = nt_dot(c[pl.ds(g * GROUP, GROUP), :], E[pl.ds(r0, RB), :])

        product(0)
        for i, (_, norms, g, r0, slot, keep) in enumerate(items):
            if i + 1 < len(items):
                product(i + 1)
            rows, cols = pl.ds(g * GROUP, GROUP), pl.ds(r0, RB)
            s = KEXP * SB[i % 2] - jnp.concatenate([norms[rows, :]] * (RB // 128), axis=1)
            m = jnp.max(s, axis=0, keepdims=True)
            p = jnp.exp2(s - m)
            LG[slot, :, cols] = m + jnp.log2(jnp.sum(p, axis=0, keepdims=True))
            if keep:
                PB[rows, cols] = p
                MG[g, :, cols] = m

    def own_items(turn, groups, starts):
        return [(CUR.at[turn], NRM, g, r0, g, True) for r0 in starts for g in groups]

    mine_at, theirs_at = range(0, ROWS, RB), range(ROWS, 2 * ROWS, RB)
    meet()
    for c in load_c:
        c.wait()
    for g in range(2):
        store_norms(NRM, CUR.at[0], g)
        store_norms(NRO, CO, g)
    mine, theirs = pl.ds(0, ROWS), pl.ds(ROWS, ROWS)

    late = []
    for turn in range(ITERS):
        last = turn == ITERS - 1
        if turn == 0:
            items = []
            for r0 in mine_at:
                items += own_items(0, range(2), [r0])
                items += [(CO, NRO, g, r0, 2 + g, False) for g in range(2)]
            run_scores(items, {})
            XS[turn] = lse2([LG[i, :, mine] for i in range(4)])
        else:
            run_scores(own_items(turn, [0], theirs_at), {})
            LOC[:, theirs] = lse2([LG[0, :, theirs], LG[1, :, theirs]])
            part = remote(LOC.at[:, theirs], SR.at[0], s_s.at[0], s_r.at[0], sib)
            part.start()
            run_scores(own_items(turn, [0], mine_at), {})
            both = lse2([LG[0, :, mine], LG[1, :, mine]])
            part.wait()
            XS[turn] = lse2([both, SR[0]])

        sends = [
            remote(XS.at[turn], XR.at[turn, k], x_s.at[turn], x_r.at[turn], cdev(k)) for k in range(NC - 1)
        ]
        for c in sends:
            c.start()
        if turn == 0:
            send_e[0].wait_recv()
            run_scores(own_items(0, range(2), theirs_at), {2: send_e[1].wait_recv})

        late.append(remote(XR.at[turn], XR.at[turn], x_s.at[turn], x_r.at[turn], sib))
        late[-1].wait_recv()
        total = lse2([XS[turn]] + [XR[turn, k] for k in range(NC - 1)])
        SS[turn] = total
        LOC[:, mine] = total
        back = remote(SS.at[turn], SR.at[1 + turn], s_s.at[1 + turn], s_r.at[1 + turn], sib)
        back.start()
        MACC[...] = jnp.zeros_like(MACC)

        def weights(r0):
            lse = LOC[:, pl.ds(r0, RB)]
            for g in range(2):
                rows = pl.ds(g * GROUP, GROUP)
                w = (PB[rows, pl.ds(r0, RB)] * jnp.exp2(MG[g, :, pl.ds(r0, RB)] - lse)).astype(BF16)
                W[rows, pl.ds(r0, RB)] = w
                wf = w.astype(F32)
                MACC[rows, :] += sum(wf[:, i * 128 : (i + 1) * 128] for i in range(RB // 128))

        def sums(q, depth, add=False):
            rows = pl.ds(q * 2 * CHUNK, 2 * CHUNK)
            v = jnp.dot(W[rows, depth], E[depth, :], preferred_element_type=F32)
            SUMS[rows, :] = SUMS[rows, :] + v if add else v

        for r0 in mine_at:
            weights(r0)
        for q in range(2):
            sums(q, mine)
        back.wait()
        LOC[:, theirs] = SR[1 + turn]
        for r0 in theirs_at:
            weights(r0)
        ring = {
            (w, c, k): remote(
                RSB.at[turn, i], RRB.at[turn, i], rs_s.at[turn], rs_r.at[turn, i],
                zdev(CHAINS[c][0] * LINKS[CHAINS[c][2]][k]),
            )
            for (w, c, k), i in MSG.items()
        }

        def ring_send(k, chains):
            for w in range(WAVES):
                for c in chains:
                    d, h, reach = CHAINS[c]
                    o = (d * SUMMED[reach][k]) % NZ
                    v = SUMS[pl.ds(SLOT[o] * CHUNK + (2 * w + h) * PIECE, PIECE), :]
                    for j in ADDS[reach][k]:
                        ring[w, c, j].wait_recv()
                        v = v + RRB[turn, MSG[w, c, j]].astype(F32)
                    RSB[turn, MSG[w, c, k]] = v.astype(BF16)
                    ring[w, c, k].start()

        sums(0, theirs, add=True)
        ring_send(0, (0, 1, 2))
        sums(1, theirs, add=True)
        ring_send(0, (3,))
        ring_send(3, (0,))
        sums(2, pl.ds(0, 2 * ROWS))
        ring_send(3, (1,))
        sums(3, pl.ds(0, 2 * ROWS))
        MS[turn] = jnp.sum(MACC[...].T, axis=0, keepdims=True)
        masses = [
            remote(MS.at[turn], MR.at[turn, h - 1], m_s.at[turn], m_r.at[turn], zdev(h)) for h in ALONG
        ]
        for c in masses:
            c.start()
        for k in (1, 2):
            ring_send(k, range(4))
        late.append(remote(MR.at[turn], MR.at[turn], m_s.at[turn], m_r.at[turn], sib))
        late[-1].wait_recv()
        lane = lax.broadcasted_iota(jnp.int32, (CHUNK, 128), 1)
        row = lax.broadcasted_iota(jnp.int32, (CHUNK, 128), 0)
        acc = jnp.zeros((CHUNK, 128), F32)
        for h in range(NZ):
            j = SLOT[h]
            vec = MS[turn] if h == 0 else MR[turn, h - 1]
            vec = vec[:, (j // 2) * 128 : (j // 2 + 1) * 128]
            acc = acc + jnp.where(lane == row + CHUNK * (j % 2), jnp.broadcast_to(vec, (CHUNK, 128)), 0.0)
        inv = 1.0 / (jnp.sum(acc, axis=1, keepdims=True) + 1.0)

        def place(o, piece):
            start = piece * PIECE
            if last:
                return out.at[pl.ds(pl.multiple_of(chunk_row(SLOT[o % NZ]) + start, PIECE), PIECE)]
            return CUR.at[turn + 1, pl.ds(SLOT[o % NZ] * CHUNK + start, PIECE)]

        gather, pairs, keeps = {}, {}, []
        for (w, c, k), i in MSG.items():
            d, h, reach = CHAINS[c]
            piece = 2 * w + h
            held, links = HELD[reach][k], LINKS[reach][k]
            src = place(-d * held, piece)
            dst = src if last else place(-d * (held + links), piece)
            if last and k == 0:
                src = CUR.at[0, pl.ds(piece * PIECE, PIECE)]
            gather[w, c, k] = remote(src, dst, ag_s.at[turn], ag_r.at[turn, i], zdev(d * links))
            if last:
                got = place(-d * (held + links), piece)
                pairs[w, c, k] = remote(got, got, o_s.at[0], o_r.at[0], sib)
        if last:
            for w in range(WAVES):
                start = 2 * w * PIECE
                fresh = CUR.at[0, pl.ds(start, 2 * PIECE)]
                rows = out.at[pl.ds(pl.multiple_of(chunk_row(SLOT[0]) + start, 2 * PIECE), 2 * PIECE)]
                pairs[w] = remote(fresh, rows, o_s.at[0], o_r.at[0], sib)
                keeps.append(pltpu.make_async_copy(fresh, rows, o_l.at[w]))

        def finish(w):
            for h in range(2):
                piece = 2 * w + h
                rows = pl.ds(SLOT[0] * CHUNK + piece * PIECE, PIECE)
                v = SUMS[rows, :] + CUR[turn, rows, :].astype(F32)
                for c in range(4):
                    if CHAINS[c][1] == h:
                        ring[w, c, 2].wait_recv()
                        v = v + RRB[turn, MSG[w, c, 2]].astype(F32)
                fresh = (v * inv[piece * PIECE : (piece + 1) * PIECE]).astype(BF16)
                if last:
                    CUR[0, pl.ds(piece * PIECE, PIECE), :] = fresh
                else:
                    CUR[turn + 1, rows, :] = fresh
                for c in range(4):
                    if CHAINS[c][1] == h:
                        gather[w, c, 0].start()
            if last:
                pairs[w].start()
                keeps[w].start()

        def gather_stage(stage):
            for w in range(WAVES):
                for c, (d, h, reach) in enumerate(CHAINS):
                    gather[w, c, stage - 1].wait_recv()
                    if stage < 3:
                        gather[w, c, stage].start()
                    if stage == 1 and reach == 4:
                        gather[w, c, 3].start()
                    if last:
                        pairs[w, c, stage - 1].start()
            if stage == 2:
                for w in range(WAVES):
                    for c in (0, 1):
                        gather[w, c, 3].wait_recv()
                        if last:
                            pairs[w, c, 3].start()

        for w in range(WAVES):
            finish(w)
        gather_stage(1)
        gather_stage(2)
        if last:
            gather_stage(3)
            row_lse[...] = (SS[turn] * LN2).reshape(ROWS)
        else:
            store_norms(NRM, CUR.at[turn + 1], 1)
            run_scores(own_items(turn + 1, [1], mine_at), {})
            run_scores(own_items(turn + 1, [1], theirs_at), {})
            gather_stage(3)
            store_norms(NRM, CUR.at[turn + 1], 0)
        late.append(remote(RSB.at[turn], RSB.at[turn], rs_s.at[turn], rs_r.at[turn, 0], sib))
        late.append(remote(RSB.at[turn], RSB.at[turn], ag_s.at[turn], ag_r.at[turn, 0], sib))

    for c in late + send_e:
        c.wait_send()
    for c in keeps:
        c.wait()
    remote(CUR.at[1], CUR.at[1], o_s.at[0], o_r.at[0], sib).wait()


def per_device(embeds, centroids):
    dma = pltpu.SemaphoreType.DMA
    new, lse = pl.pallas_call(
        kernel,
        out_shape=(
            jax.ShapeDtypeStruct((CENTS, D), BF16),
            jax.ShapeDtypeStruct((ROWS,), F32),
        ),
        in_specs=[pl.BlockSpec(memory_space=pltpu.HBM)] * 2,
        out_specs=(pl.BlockSpec(memory_space=pl.ANY), pl.BlockSpec(memory_space=pltpu.VMEM)),
        scratch_shapes=[
            pltpu.VMEM((2 * ROWS, D), BF16),
            pltpu.VMEM((ITERS, OWN, D), BF16),
            pltpu.VMEM((OWN, D), BF16),
            pltpu.VMEM((OWN, 128), F32),
            pltpu.VMEM((OWN, 128), F32),
            pltpu.VMEM((OWN, 2 * ROWS), F32),
            pltpu.VMEM((OWN, 2 * ROWS), BF16),
            pltpu.VMEM((OWN, D), F32),
            pltpu.VMEM((2, GROUP, RB), F32),
            pltpu.VMEM((2, 1, 2 * ROWS), F32),
            pltpu.VMEM((4, 1, 2 * ROWS), F32),
            pltpu.VMEM((1, 2 * ROWS), F32),
            pltpu.VMEM((ITERS, 1, ROWS), F32),
            pltpu.VMEM((ITERS, NC - 1, 1, ROWS), F32),
            pltpu.VMEM((ITERS, 1, ROWS), F32),
            pltpu.VMEM((ITERS + 1, 1, ROWS), F32),
            pltpu.VMEM((OWN, 128), F32),
            pltpu.VMEM((ITERS, 1, OWN), F32),
            pltpu.VMEM((ITERS, NZ - 1, 1, OWN), F32),
            pltpu.VMEM((ITERS, NMSG, PIECE, D), BF16),
            pltpu.VMEM((ITERS, NMSG, PIECE, D), BF16),
            dma((ROWS // RB,)),
            dma((NZ + 1,)),
            dma((ROWS // RB,)),
            dma((ROWS // RB,)),
            dma((ITERS,)),
            dma((ITERS,)),
            dma((ITERS + 1,)),
            dma((ITERS + 1,)),
            dma((ITERS,)),
            dma((ITERS,)),
            dma((ITERS,)),
            dma((ITERS, NMSG)),
            dma((ITERS,)),
            dma((ITERS, NMSG)),
            dma((WAVES,)),
            dma((1,)),
            dma((1,)),
        ],
        compiler_params=pltpu.CompilerParams(
            collective_id=0, has_side_effects=True, vmem_limit_bytes=50 * 1024 * 1024
        ),
    )(embeds, centroids)
    return new, lse


def solution(mesh):
    return jax.shard_map(
        per_device,
        mesh=mesh,
        in_specs=(P("dp", None), P("cent", None)),
        out_specs=(P("cent", None), P("dp")),
        check_vma=False,
    )
```
